256 devices in a mesh: tm: 64 (over x, z, y_lo), sx: 2 (over core), sy: 2 (over y_hi).
Axes of the slice: x: 4, y: 4 (y_hi: 2, y_lo: 2; y = y_hi * 2 + y_lo), z: 8, core: 2. Of those that a mesh axis runs over, the one named last changes fastest.
Arguments:
- initial_states: float32 [64, 8, 64, 256], P('tm', None, 'sx', 'sy'), may hold values from -6 to 6
- coarse_decay: float32 [64, 8, 64, 256], P('tm', None, 'sx', 'sy'), may hold values from 0 to 1, as said below
- power_map: float32 [8, 64, 256], P(None, 'sx', 'sy'), may hold values from 0.5 to 2
- power_mask: int32 [64, 4, 8], P('tm'), may hold values 0 or 1
- region_ids: int32 [8, 8], replicated, may hold values from 0 to 3
- region_conductivity: float32 [4], replicated, may hold values from 0.4 to 2.5
Outputs:
- cycle_states: float32 [64, 8, 64, 256], P('tm', None, 'sx', 'sy')
- jump_field: float32 [64, 8, 64, 256], P('tm', None, 'sx', 'sy')
The draws below stay inside these ranges and needn't reach their ends.
Inputs may be any that keep to these rules, and one draw needn't show every extreme that they name: `coarse_decay`: every entry lies between 0 and 1, and for every cell the product of its 64 factors is at most one half.
All inputs are finite; a program needn't handle non-finite values. No bound on the sum of `power_mask` on one device may be relied on, other than what follows from the above.
Results may differ from the reference program's by a relative error of at most 0.0001.
Values sent between devices are 32-bit elements; how exact they have to be, the bound alone decides.
No kernel may reach another device: no remote copies, remote signals or barrier semaphores. Data moves between devices by JAX's collectives and lax.ppermute only.
A program may use at most 128 MiB of HBM per device.

```python
import math
import jax
import jax.numpy as jnp
from jax import lax

LAYERS = 8
RB = 8
REGIONS = 4
FSTEPS = 4
SWEEPS = 3
ITERS = 2
TIME_SLABS = 64
NX = 64
NY = 256
ROWBLOCKS = 8


def draw_coarse_decay(key, part):
    key_pick, key_fast, key_slow, key_strike_points, key_split_points = jax.random.split(key, 5)
    array_extent = (TIME_SLABS, LAYERS, NX, NY)
    share = 0.5
    slow_cells = jax.random.uniform(key_pick, (1, LAYERS, NX, NY), jnp.float32) < share
    fast_rate = jnp.exp(jax.random.uniform(key_fast, array_extent, jnp.float32, jnp.log(0.02), jnp.log(0.5)))
    slow_power = jax.random.uniform(key_slow, array_extent, jnp.float32, 0.32, 1.0)
    gradual_decline = jnp.exp(jnp.log(0.1) * slow_power / TIME_SLABS)
    pulse_strikes = jax.random.uniform(key_strike_points, array_extent, jnp.float32) < 3.0 / TIME_SLABS
    pulse_splits = jax.random.uniform(key_split_points, array_extent, jnp.float32, 0.5, 0.8)
    gradual_decline = jnp.where(pulse_strikes, gradual_decline * pulse_splits, gradual_decline)
    return jnp.where(slow_cells, gradual_decline, fast_rate).astype(jnp.float32)


def touch_ends(array, key, smallest, top_value):
    spot = [jax.random.randint(jax.random.fold_in(key, axis), (), 0, length) for axis, length in enumerate(array.shape)]
    longest = array.shape.index(max(array.shape))
    beside = spot[:longest] + [(spot[longest] + 1) % array.shape[longest]] + spot[longest + 1:]
    return array.at[tuple(spot)].set(smallest).at[tuple(beside)].set(top_value)


def level_of(stream_key, extent, cuts, low, largest):
    level, own = 1.0, jax.random.fold_in(stream_key, 6)
    for position, parts in cuts:
        steps = jnp.exp(jax.random.uniform(jax.random.fold_in(own, position), (parts,), jnp.float32, low / len(cuts), largest / len(cuts)))
        level = level * jnp.repeat(steps, extent[position] // parts).reshape([-1 if axis == position else 1 for axis in range(len(extent))])
    return level


def noise(key, extent, deviation, bound, cuts=(), kind=jnp.bfloat16):
    values = deviation * jax.random.normal(key, extent, jnp.float32)
    if cuts:
        values = values * level_of(key, extent, cuts, -0.22, 0.18)
    return jnp.clip(values, -bound, bound).astype(kind)


def setup_inputs(seed: int = 0) -> dict:
    keys = jax.random.split(jax.random.key(seed), 7)
    return {
        "initial_states": noise(keys[0], (TIME_SLABS, LAYERS, NX, NY), 1.0, 6.0, ((0, 64), (2, 2), (3, 2)), jnp.float32),
        "coarse_decay": draw_coarse_decay(jax.random.fold_in(keys[6], 71), 0),
        "power_map": jnp.clip(jnp.exp(math.log(2.0) - 1.3862944 * jax.random.uniform(keys[2], (LAYERS, NX, NY), jnp.float32) ** level_of(keys[2], (LAYERS, NX, NY), ((1, 2), (2, 2)), -0.2, 0.2)), 0.5, 2.0),
        "power_mask": touch_ends((jax.random.randint(keys[3], (TIME_SLABS, FSTEPS, ROWBLOCKS), 0, 2) < 1).astype(jnp.int32), jax.random.fold_in(keys[3], 1), 0, 1),
        "region_ids": touch_ends(jax.random.randint(keys[4], (LAYERS, ROWBLOCKS), 0, REGIONS), jax.random.fold_in(keys[4], 1), 0, REGIONS - 1).astype(jnp.int32),
        "region_conductivity": jnp.clip(jnp.exp(jax.random.uniform(keys[5], (REGIONS,), jnp.float32, math.log(0.4), math.log(2.5))), 0.4, 2.5),
    }


grid_xy = 1.0
grid_z = 0.5
sink_gain = 0.5
source_gain = 0.5
cond_slope = 0.25
joule_slope = 0.3


def base_rows(region_ids, region_conductivity):
    labels = jnp.arange(REGIONS, dtype=jnp.int32)
    chosen = (region_ids[:, :, None] == labels[None, None, :]).astype(jnp.float32)
    return jnp.sum(chosen * region_conductivity[None, None, :], axis=2)


def face_weights(cond_pad, weight_scale):
    middle = cond_pad[:, 1:-1, 1:-1]
    layer_index = lax.broadcasted_iota(jnp.int32, middle.shape, 0)
    blank_layer = jnp.zeros_like(middle[:1])
    layer_above = jnp.concatenate([middle[1:], blank_layer], axis=0)
    layer_below = jnp.concatenate([blank_layer, middle[:-1]], axis=0)
    weight_west = weight_scale * (grid_xy * (0.5 * (middle + cond_pad[:, :-2, 1:-1])))
    weight_east = weight_scale * (grid_xy * (0.5 * (middle + cond_pad[:, 2:, 1:-1])))
    weight_south = weight_scale * (grid_xy * (0.5 * (middle + cond_pad[:, 1:-1, :-2])))
    weight_north = weight_scale * (grid_xy * (0.5 * (middle + cond_pad[:, 1:-1, 2:])))
    weight_up = jnp.where(layer_index == middle.shape[0] - 1, jnp.zeros_like(middle), weight_scale * (grid_z * (0.5 * (middle + layer_above))))
    weight_down = jnp.where(layer_index == 0, weight_scale * (sink_gain * middle), weight_scale * (grid_z * (0.5 * (middle + layer_below))))
    denominator = 1.0 + (((((weight_west + weight_east) + weight_south) + weight_north) + weight_down) + weight_up)
    return (weight_west, weight_east, weight_south, weight_north, weight_down, weight_up), denominator


def relax(padded, weights, right_side, denominator):
    weight_west, weight_east, weight_south, weight_north, weight_down, weight_up = weights
    middle = padded[:, 1:-1, 1:-1]
    blank_layer = jnp.zeros_like(middle[:1])
    layer_above = jnp.concatenate([middle[1:], blank_layer], axis=0)
    layer_below = jnp.concatenate([blank_layer, middle[:-1]], axis=0)
    summed = weight_west * padded[:, :-2, 1:-1] + weight_east * padded[:, 2:, 1:-1]
    summed = summed + weight_south * padded[:, 1:-1, :-2] + weight_north * padded[:, 1:-1, 2:]
    summed = summed + weight_down * layer_below + weight_up * layer_above
    return (right_side + summed) / denominator


def fine_slab(initial, mask_rows, base_cond, power_map):
    current = initial
    previous = initial
    for substep in range(FSTEPS):
        if substep == 0:
            coef_now, coef_old, weight_scale = 1.0, 0.0, 1.0
        else:
            coef_now, coef_old, weight_scale = 4.0 / 3.0, -1.0 / 3.0, 2.0 / 3.0
        conductance = base_cond[:, :, None] * (1.0 - cond_slope * jnp.tanh(current))
        cond_pad = jnp.pad(conductance, ((0, 0), (1, 1), (1, 1)))
        weights, denominator = face_weights(cond_pad, weight_scale)
        heat_source = source_gain * mask_rows[substep][None, :, None] * power_map * (1.0 + joule_slope * jnp.tanh(current))
        right_side = coef_now * current + coef_old * previous + weight_scale * heat_source
        iterate = current
        for sweep_index in range(SWEEPS):
            iterate = relax(jnp.pad(iterate, ((0, 0), (1, 1), (1, 1))), weights, right_side, denominator)
        previous = current
        current = iterate
    return current


def periodic_solve(decay_rate, offset):
    def advance(running, slab_item):
        scale_sum, shift_sum = running
        rate_now, offset_now = slab_item
        return (scale_sum * rate_now, rate_now * shift_sum + offset_now), (scale_sum, shift_sum)

    unit_map = jnp.ones(decay_rate.shape[1:], jnp.float32)
    zero_map = jnp.zeros(decay_rate.shape[1:], jnp.float32)
    totals, prefixes = lax.scan(advance, (unit_map, zero_map), (decay_rate, offset))
    scale_total, shift_total = totals
    scale_pre, shift_pre = prefixes
    first_state = shift_total / (1.0 - scale_total)
    return scale_pre * first_state[None] + shift_pre


def reference(initial_states, coarse_decay, power_map, power_mask, region_ids, region_conductivity):
    base_cond = jnp.repeat(base_rows(region_ids, region_conductivity), RB, axis=1)
    mask_rows = jnp.repeat(power_mask.astype(jnp.float32), RB, axis=2)

    def fine_all(states):
        return lax.map(lambda bundle: fine_slab(bundle[0], bundle[1], base_cond, power_map), (states, mask_rows))

    states = initial_states
    jump_field = jnp.zeros_like(initial_states)
    for round_index in range(ITERS):
        fine_end = fine_all(states)
        if round_index == ITERS - 1:
            jump_field = fine_end - jnp.roll(states, -1, axis=0)
        offset = fine_end - coarse_decay * states
        states = periodic_solve(coarse_decay, offset)
    return states, jump_field
```

```python
import functools

import jax
import jax.numpy as jnp
from jax import lax
from jax.experimental import pallas as pl
from jax.experimental.pallas import tpu as pltpu
from jax.sharding import PartitionSpec as P

RB = 8
REGIONS = 4
FSTEPS = 4
SWEEPS = 3
ITERS = 2
cond_slope = 0.25
joule_slope = 0.3

HALO = FSTEPS * SWEEPS
ROWS = 32
LAYERS = 8
COLS = 128
BOX = ROWS + HALO
GROUPS = 3
PACK = 15
WIDE = 40
VMEM = pltpu.VMEM


def spec():
    return pl.BlockSpec(memory_space=VMEM)


def sspec():
    return pl.BlockSpec(memory_space=pltpu.SMEM)


def plane(*shape):
    return jax.ShapeDtypeStruct((*shape, LAYERS, COLS), jnp.float32)


def lanes():
    return lax.broadcasted_iota(jnp.int32, (LAYERS, COLS), 1)


def layers():
    return lax.broadcasted_iota(jnp.int32, (LAYERS, COLS), 0)


def box_row(r, own, halo):
    r = min(r, BOX - 1)
    return own[r] if r < ROWS else halo[BOX - 1 - r]


def packed_row(i, row, shift):
    lane = lanes()
    parts = [pltpu.roll(row(g * PACK + i), shift + g * WIDE, 1) for g in range(GROUPS)]
    return jnp.where(lane < WIDE, parts[0], jnp.where(lane < 2 * WIDE, parts[1], parts[2]))


def own_shift(sy):
    return jnp.where(sy == 0, 24, 12)


def sent_shift(sy):
    return jnp.where(sy == 0, 12, 24)


def advance(n, packed, state, tmp, wx, wyp, wzp, inv, rhs, base, heat, power):
    lane = lanes()
    layer = layers()
    edge = jnp.where(layer == 0, 1.0, 0.0)
    if not packed:
        edge = edge + jnp.where(lane == 0, 1.0, 0.0) + jnp.where(lane == COLS - 1, 1.0, 0.0)

    def step(m, carry):
        first = m == 0
        now = lax.rem(m, 2)
        old = 1 - now
        coef_now = jnp.where(first, 1.0, 4.0 / 3.0).astype(jnp.float32)
        coef_old = jnp.where(first, 0.0, -1.0 / 3.0).astype(jnp.float32)
        half = jnp.where(first, 0.5, 1.0 / 3.0).astype(jnp.float32)
        cond = []
        for r in range(n):
            cur = state[now, r]
            tanh = jnp.tanh(cur)
            cond.append((half * base(r)) * (1.0 - cond_slope * tanh))
            source = (half * heat(m, r)) * power[r] * (1.0 + joule_slope * tanh)
            rhs[r] = coef_now * cur + coef_old * state[old, r] + source
        faces = []
        for r in range(n):
            if r:
                faces.append(cond[r - 1] + cond[r])
            elif packed:
                faces.append(jnp.where(lane < WIDE, 0.0, cond[0] + pltpu.roll(cond[n - 1], WIDE, 1)))
            else:
                faces.append(None)
        faces.append(cond[n - 1] + pltpu.roll(cond[0], COLS - WIDE, 1) if packed else None)
        for r in range(n + 1):
            if faces[r] is not None:
                wx[r] = faces[r]
        for r in range(n):
            c = cond[r]
            north = c + pltpu.roll(c, COLS - 1, 1)
            if not packed:
                north = jnp.where(lane == COLS - 1, 0.0, north)
            up = jnp.where(layer == LAYERS - 1, 0.0, 0.5 * (c + pltpu.roll(c, LAYERS - 1, 0)))
            total = north + pltpu.roll(north, 1, 1) + up + pltpu.roll(up, 1, 0) + edge * c
            low = faces[r]
            if r == 0:
                low = c if low is None else low + jnp.where(lane < WIDE, c, 0.0)
            high = c if faces[r + 1] is None else faces[r + 1]
            wyp[r] = north
            wzp[r] = up
            inv[r] = 1.0 / (1.0 + (total + low + high))

        def sweep(source, store):
            vs = [source(r) for r in range(n)]
            for r in range(n):
                v = vs[r]
                north = wyp[r]
                up = wzp[r]
                acc = rhs[r] + pltpu.roll(north * v, 1, 1) + north * pltpu.roll(v, COLS - 1, 1)
                acc = acc + pltpu.roll(up * v, 1, 0) + up * pltpu.roll(v, LAYERS - 1, 0)
                if r:
                    acc = acc + wx[r] * vs[r - 1]
                elif packed:
                    acc = acc + wx[0] * pltpu.roll(vs[n - 1], WIDE, 1)
                if r < n - 1:
                    acc = acc + wx[r + 1] * vs[r + 1]
                elif packed:
                    acc = acc + wx[n] * pltpu.roll(vs[0], COLS - WIDE, 1)
                store(r, acc * inv[r])

        def into(ref, *at):
            def put(r, value):
                ref[(*at, r)] = value
            return put

        sweep(lambda r: state[now, r], into(tmp, 0))
        sweep(lambda r: tmp[0, r], into(tmp, 1))
        sweep(lambda r: tmp[1, r], into(state, old))
        return carry

    lax.fori_loop(0, FSTEPS, step, 0)


def scratch(n):
    return [VMEM((2, n, LAYERS, COLS), jnp.float32), VMEM((2, n, LAYERS, COLS), jnp.float32)] + [
        VMEM((n + 1, LAYERS, COLS), jnp.float32) for _ in range(5)
    ]


def native_row(here, r):
    return jnp.where(here[0] == 0, r, ROWS - 1 - r)


def turn_kernel(count, here, *refs):
    ins, outs, send = refs[:count], refs[count:2 * count], refs[2 * count]
    for k in range(count):
        for r in range(ROWS):
            row = ins[k][pl.ds(native_row(here, r), LAYERS, stride=ROWS), :]
            outs[k][r] = row
            if r >= ROWS - HALO:
                send[k, r - (ROWS - HALO)] = row


def turn(here, arrays):
    count = len(arrays)
    return pl.pallas_call(
        functools.partial(turn_kernel, count),
        out_shape=[plane(ROWS)] * count + [plane(count, HALO)],
        in_specs=[sspec()] + [spec()] * count,
        out_specs=[spec()] * (count + 1),
        name="turn",
    )(here, *[a.reshape(LAYERS * ROWS, COLS) for a in arrays])


def pack_kernel(count, here, *refs):
    owns, halo, out = refs[:count], refs[count], refs[count + 1]
    shift = sent_shift(here[1])
    for k in range(count):
        for i in range(PACK):
            out[k, i] = packed_row(i, lambda r: box_row(r, owns[k], halo.at[k]), shift)


def pack(here, owns, halo):
    count = len(owns)
    return pl.pallas_call(
        functools.partial(pack_kernel, count),
        out_shape=plane(count, PACK),
        in_specs=[sspec()] + [spec()] * (count + 1),
        out_specs=spec(),
        name="pack",
    )(here, *owns, halo)


def main_kernel(first, here, mask, base, own, halo, *refs):
    if first:
        power_own, decay, end, band, power_box, power_band, decay_box, *work = refs
        for r in range(BOX):
            power_box[r] = box_row(r, power_own, halo.at[1])
        for r in range(ROWS):
            decay_box[r] = decay[pl.ds(native_row(here, r), LAYERS, stride=ROWS), :]
    else:
        power_box, end, band, *work = refs
    state = work[0]
    shift = own_shift(here[1])
    for r in range(BOX):
        row = box_row(r, own, halo.at[0])
        state[0, r] = row
        state[1, r] = row
    for i in range(PACK):
        band[i] = packed_row(i, lambda r: box_row(r, own, halo.at[0]), shift)
        if first:
            power_band[i] = packed_row(i, lambda r: box_row(r, power_own, halo.at[1]), shift)
    advance(
        BOX, False, *work,
        lambda r: base[r // RB],
        lambda m, r: mask[m, r // RB],
        power_box,
    )
    for r in range(ROWS):
        end[r] = state[0, r]


def main(here, mask, base, own, halo, first, extra):
    outs = [plane(ROWS), plane(PACK)]
    if first:
        outs = outs + [plane(BOX), plane(PACK), plane(ROWS)]
    return pl.pallas_call(
        functools.partial(main_kernel, first),
        out_shape=outs,
        in_specs=[sspec(), sspec()] + [spec()] * (3 + len(extra)),
        out_specs=[spec()] * len(outs),
        scratch_shapes=scratch(BOX),
        cost_estimate=pl.CostEstimate(flops=20_000_000, bytes_accessed=4_000_000, transcendentals=400_000),
        name="propagate_rows",
    )(here, mask, base, own, halo, *extra)


def band_kernel(first, here, mask, base, end, band, other, own, decay, *refs):
    if first:
        power_own, power, offset_box, send, *work = refs
    else:
        power, offset_before, send, jump, *work = refs
    state = work[0]
    lane = lanes()
    slot = lane - jnp.where(lane < WIDE, 0, jnp.where(lane < 2 * WIDE, WIDE, 2 * WIDE))
    left = here[1] == 0
    here_low = jnp.where(left, 0, 12)
    here_high = jnp.where(left, 24, 36)
    mine = (slot >= here_low) & (slot < here_high)
    for i in range(PACK):
        row = jnp.where(mine, band[i], other[0, i])
        state[0, i] = row
        state[1, i] = row
        if first:
            power[i] = jnp.where(mine, power_own[i], other[1, i])

    def by_group(value):
        return jnp.where(lane < WIDE, value(0), jnp.where(lane < 2 * WIDE, value(1), value(2)))

    def block(g, i):
        return min(g * PACK + i, BOX - 1) // RB

    advance(
        PACK, True, *work,
        lambda i: by_group(lambda g: base[block(g, i)]),
        lambda m, i: by_group(lambda g: mask[m, block(g, i)]),
        power,
    )
    back = COLS - own_shift(here[1])
    border = ((lane >= COLS - HALO) & left) | ((lane < HALO) & jnp.logical_not(left))
    for r in range(ROWS):
        moved = pltpu.roll(state[0, r % PACK], lax.rem(back + (2 * COLS - (r // PACK) * WIDE), COLS), 1)
        f = jnp.where(border, moved, end[r])
        u = own[r]
        d = decay[r]
        x = native_row(here, r)
        if first:
            offset = f - d * u
            offset_box[r] = offset
            at = lax.div(x, 4) * 8 + lax.rem(x, 4)
            send[pl.ds(at, LAYERS, stride=64), :] = d
            send[pl.ds(at + 4, LAYERS, stride=64), :] = offset
        else:
            du = d * u
            send[pl.ds(x, LAYERS, stride=ROWS), :] = f - du
            jump[pl.ds(x, LAYERS, stride=ROWS), :] = f - (du + offset_before[r])


def border(here, mask, base, end, band, other, own, decay, first, extra):
    if first:
        outs = [plane(PACK), plane(ROWS), jax.ShapeDtypeStruct((512, COLS), jnp.float32)]
    else:
        outs = [jax.ShapeDtypeStruct((256, COLS), jnp.float32)] * 2
    return pl.pallas_call(
        functools.partial(band_kernel, first),
        out_shape=outs,
        in_specs=[sspec(), sspec()] + [spec()] * (6 + len(extra)),
        out_specs=[spec()] * len(outs),
        scratch_shapes=scratch(PACK),
        name="propagate_band",
    )(here, mask, base, end, band, other, own, decay, *extra)


def cycle_kernel(slabs, rate, offset, out):
    scale = rate(0)
    shift = offset(0)
    for k in range(1, slabs):
        d = rate(k)
        scale = scale * d
        shift = d * shift + offset(k)
    u = shift / (1.0 - scale)
    out[0] = u
    for k in range(slabs - 1):
        u = rate(k) * u + offset(k)
        out[k + 1] = u


def cycle_first(slabs, both, out):
    cycle_kernel(slabs, lambda k: both[k, 0:4], lambda k: both[k, 4:8], out)


def cycle_later(slabs, both, offset, out):
    cycle_kernel(slabs, lambda k: both[k, 0:4], lambda k: offset[k], out)


def cycle(both, offset):
    slabs = both.shape[0]
    args = (both,) if offset is None else (both, offset)
    return pl.pallas_call(
        functools.partial(cycle_first if offset is None else cycle_later, slabs),
        out_shape=jax.ShapeDtypeStruct((slabs, 4, COLS), jnp.float32),
        in_specs=[spec()] * len(args),
        out_specs=spec(),
        name="cycle",
    )(*args)


def base_rows(region_ids, region_conductivity):
    labels = jnp.arange(REGIONS, dtype=jnp.int32)
    chosen = (region_ids[:, :, None] == labels[None, None, :]).astype(jnp.float32)
    return jnp.sum(chosen * region_conductivity[None, None, :], axis=2)


SWAP = [(0, 1), (1, 0)]


def shards(initial_states, coarse_decay, power_map, power_mask, region_ids, region_conductivity):
    slabs = lax.axis_size("tm")
    sx = lax.axis_index("sx")
    here = jnp.stack([sx, lax.axis_index("sy")]).astype(jnp.int32)
    per_block = base_rows(region_ids, region_conductivity).T
    per_block = jnp.where(sx == 0, per_block, per_block[::-1])
    base = jnp.broadcast_to(per_block[:, :, None], (*per_block.shape, COLS))
    mask = power_mask[0].astype(jnp.float32)
    mask = jnp.where(sx == 0, mask, mask[:, ::-1])
    decay_native = coarse_decay.reshape(LAYERS * ROWS, COLS)

    own, power_own, send = turn(here, [initial_states, power_map])
    halo = lax.ppermute(send, "sx", SWAP)
    sent = pack(here, [own, power_own], halo)
    other = lax.ppermute(sent, "sy", SWAP)
    end, band, power_box, power_band_own, decay = main(
        here, mask, base, own, halo, True, (power_own, decay_native)
    )
    power_band, offset, both = border(
        here, mask, base, end, band, other, own, decay, True, (power_band_own,)
    )
    both = lax.all_to_all(both.reshape(slabs, 8, COLS), "tm", 0, 0, tiled=True)
    states = lax.all_to_all(cycle(both, None), "tm", 0, 0, tiled=True)

    own, send = turn(here, [states])
    halo = lax.ppermute(send, "sx", SWAP)
    sent = pack(here, [own], halo)
    other = lax.ppermute(sent, "sy", SWAP)
    end, band = main(here, mask, base, own, halo, False, (power_box,))
    later, jump = border(
        here, mask, base, end, band, other, own, decay, False, (power_band, offset)
    )
    later = lax.all_to_all(later.reshape(slabs, 4, COLS), "tm", 0, 0, tiled=True)
    states = lax.all_to_all(cycle(both, later), "tm", 0, 0, tiled=True)
    shape = (1, LAYERS, ROWS, COLS)
    return states.reshape(shape), jump.reshape(shape)


def solution(mesh):
    return jax.shard_map(
        shards,
        mesh=mesh,
        in_specs=(
            P("tm", None, "sx", "sy"),
            P("tm", None, "sx", "sy"),
            P(None, "sx", "sy"),
            P("tm", None, None),
            P(),
            P(),
        ),
        out_specs=(P("tm", None, "sx", "sy"), P("tm", None, "sx", "sy")),
        check_vma=False,
    )
```

```python
import functools

import jax
import jax.numpy as jnp
from jax import lax
from jax.experimental import pallas as pl
from jax.experimental.pallas import tpu as pltpu
from jax.sharding import PartitionSpec as P

RB = 8
REGIONS = 4
FSTEPS = 4
SWEEPS = 3
ITERS = 2
cond_slope = 0.25
joule_slope = 0.3

HALO = FSTEPS * SWEEPS
ROWS = 32
LAYERS = 8
COLS = 128
BOX = ROWS + HALO
GROUPS = 3
PACK = 15
WIDE = 40
VMEM = pltpu.VMEM


def spec():
    return pl.BlockSpec(memory_space=VMEM)


def sspec():
    return pl.BlockSpec(memory_space=pltpu.SMEM)


def plane(*shape):
    return jax.ShapeDtypeStruct((*shape, LAYERS, COLS), jnp.float32)


def lanes():
    return lax.broadcasted_iota(jnp.int32, (LAYERS, COLS), 1)


def layers():
    return lax.broadcasted_iota(jnp.int32, (LAYERS, COLS), 0)


def box_row(r, own, halo):
    r = min(r, BOX - 1)
    return own[r] if r < ROWS else halo[BOX - 1 - r]


def packed_row(i, row, shift):
    lane = lanes()
    parts = [pltpu.roll(row(g * PACK + i), shift + g * WIDE, 1) for g in range(GROUPS)]
    return jnp.where(lane < WIDE, parts[0], jnp.where(lane < 2 * WIDE, parts[1], parts[2]))


def own_shift(sy):
    return jnp.where(sy == 0, 24, 12)


def sent_shift(sy):
    return jnp.where(sy == 0, 12, 24)


def advance(n, packed, state, tmp, wx, wyp, wzp, inv, rhs, base, heat, power):
    lane = lanes()
    layer = layers()
    edge = jnp.where(layer == 0, 1.0, 0.0)
    if not packed:
        edge = edge + jnp.where(lane == 0, 1.0, 0.0) + jnp.where(lane == COLS - 1, 1.0, 0.0)

    def step(m, carry):
        first = m == 0
        now = lax.rem(m, 2)
        old = 1 - now
        coef_now = jnp.where(first, 1.0, 4.0 / 3.0).astype(jnp.float32)
        coef_old = jnp.where(first, 0.0, -1.0 / 3.0).astype(jnp.float32)
        half = jnp.where(first, 0.5, 1.0 / 3.0).astype(jnp.float32)
        cond = []
        for r in range(n):
            cur = state[now, r]
            tanh = jnp.tanh(cur)
            cond.append((half * base(r)) * (1.0 - cond_slope * tanh))
            source = (half * heat(m, r)) * power[r] * (1.0 + joule_slope * tanh)
            rhs[r] = coef_now * cur + coef_old * state[old, r] + source
        faces = []
        for r in range(n):
            if r:
                faces.append(cond[r - 1] + cond[r])
            elif packed:
                faces.append(jnp.where(lane < WIDE, 0.0, cond[0] + pltpu.roll(cond[n - 1], WIDE, 1)))
            else:
                faces.append(None)
        faces.append(cond[n - 1] + pltpu.roll(cond[0], COLS - WIDE, 1) if packed else None)
        for r in range(n + 1):
            if faces[r] is not None:
                wx[r] = faces[r]
        for r in range(n):
            c = cond[r]
            north = c + pltpu.roll(c, COLS - 1, 1)
            if not packed:
                north = jnp.where(lane == COLS - 1, 0.0, north)
            up = jnp.where(layer == LAYERS - 1, 0.0, 0.5 * (c + pltpu.roll(c, LAYERS - 1, 0)))
            total = north + pltpu.roll(north, 1, 1) + up + pltpu.roll(up, 1, 0) + edge * c
            low = faces[r]
            if r == 0:
                low = c if low is None else low + jnp.where(lane < WIDE, c, 0.0)
            high = c if faces[r + 1] is None else faces[r + 1]
            wyp[r] = north
            wzp[r] = up
            inv[r] = 1.0 / (1.0 + (total + low + high))

        def sweep(source, store):
            vs = [source(r) for r in range(n)]
            for r in range(n):
                v = vs[r]
                north = wyp[r]
                up = wzp[r]
                acc = rhs[r] + pltpu.roll(north * v, 1, 1) + north * pltpu.roll(v, COLS - 1, 1)
                acc = acc + pltpu.roll(up * v, 1, 0) + up * pltpu.roll(v, LAYERS - 1, 0)
                if r:
                    acc = acc + wx[r] * vs[r - 1]
                elif packed:
                    acc = acc + wx[0] * pltpu.roll(vs[n - 1], WIDE, 1)
                if r < n - 1:
                    acc = acc + wx[r + 1] * vs[r + 1]
                elif packed:
                    acc = acc + wx[n] * pltpu.roll(vs[0], COLS - WIDE, 1)
                store(r, acc * inv[r])

        def into(ref, *at):
            def put(r, value):
                ref[(*at, r)] = value
            return put

        sweep(lambda r: state[now, r], into(tmp, 0))
        sweep(lambda r: tmp[0, r], into(tmp, 1))
        sweep(lambda r: tmp[1, r], into(state, old))
        return carry

    lax.fori_loop(0, FSTEPS, step, 0)


def scratch(n):
    return [VMEM((2, n, LAYERS, COLS), jnp.float32), VMEM((2, n, LAYERS, COLS), jnp.float32)] + [
        VMEM((n + 1, LAYERS, COLS), jnp.float32) for _ in range(5)
    ]


def native_row(here, r):
    return jnp.where(here[0] == 0, r, ROWS - 1 - r)


def turn_kernel(count, here, *refs):
    ins, outs, send = refs[:count], refs[count:2 * count], refs[2 * count]
    for k in range(count):
        for r in range(ROWS):
            row = ins[k][pl.ds(native_row(here, r), LAYERS, stride=ROWS), :]
            outs[k][r] = row
            if r >= ROWS - HALO:
                send[k, r - (ROWS - HALO)] = row


def turn(here, arrays):
    count = len(arrays)
    return pl.pallas_call(
        functools.partial(turn_kernel, count),
        out_shape=[plane(ROWS)] * count + [plane(count, HALO)],
        in_specs=[sspec()] + [spec()] * count,
        out_specs=[spec()] * (count + 1),
        compiler_params=pltpu.CompilerParams(vmem_limit_bytes=8 * 1024 * 1024),
        name="turn",
    )(here, *[a.reshape(LAYERS * ROWS, COLS) for a in arrays])


def pack_kernel(count, here, *refs):
    owns, halo, out = refs[:count], refs[count], refs[count + 1]
    shift = sent_shift(here[1])
    for k in range(count):
        for i in range(PACK):
            out[k, i] = packed_row(i, lambda r: box_row(r, owns[k], halo.at[k]), shift)


def pack(here, owns, halo):
    count = len(owns)
    return pl.pallas_call(
        functools.partial(pack_kernel, count),
        out_shape=plane(count, PACK),
        in_specs=[sspec()] + [spec()] * (count + 1),
        out_specs=spec(),
        compiler_params=pltpu.CompilerParams(vmem_limit_bytes=8 * 1024 * 1024),
        name="pack",
    )(here, *owns, halo)


def main_kernel(first, here, mask, base, own, halo, *refs):
    if first:
        power_own, decay, end, band, power_box, power_band, decay_box, *work = refs
        for r in range(BOX):
            power_box[r] = box_row(r, power_own, halo.at[1])
        for r in range(ROWS):
            decay_box[r] = decay[pl.ds(native_row(here, r), LAYERS, stride=ROWS), :]
    else:
        power_box, end, band, *work = refs
    state = work[0]
    shift = own_shift(here[1])
    for r in range(BOX):
        row = box_row(r, own, halo.at[0])
        state[0, r] = row
        state[1, r] = row
    for i in range(PACK):
        band[i] = packed_row(i, lambda r: box_row(r, own, halo.at[0]), shift)
        if first:
            power_band[i] = packed_row(i, lambda r: box_row(r, power_own, halo.at[1]), shift)
    advance(
        BOX, False, *work,
        lambda r: base[r // RB],
        lambda m, r: mask[m, r // RB],
        power_box,
    )
    for r in range(ROWS):
        end[r] = state[0, r]


def main(here, mask, base, own, halo, first, extra):
    outs = [plane(ROWS), plane(PACK)]
    if first:
        outs = outs + [plane(BOX), plane(PACK), plane(ROWS)]
    return pl.pallas_call(
        functools.partial(main_kernel, first),
        out_shape=outs,
        in_specs=[sspec(), sspec()] + [spec()] * (3 + len(extra)),
        out_specs=[spec()] * len(outs),
        scratch_shapes=scratch(BOX),
        cost_estimate=pl.CostEstimate(flops=20_000_000, bytes_accessed=4_000_000, transcendentals=400_000),
        compiler_params=pltpu.CompilerParams(vmem_limit_bytes=8 * 1024 * 1024),
        name="propagate_rows",
    )(here, mask, base, own, halo, *extra)


def band_kernel(first, here, mask, base, end, band, other, own, decay, *refs):
    if first:
        power_own, power, offset_box, send, *work = refs
    else:
        power, offset_before, send, jump, *work = refs
    state = work[0]
    lane = lanes()
    slot = lane - jnp.where(lane < WIDE, 0, jnp.where(lane < 2 * WIDE, WIDE, 2 * WIDE))
    left = here[1] == 0
    here_low = jnp.where(left, 0, 12)
    here_high = jnp.where(left, 24, 36)
    mine = (slot >= here_low) & (slot < here_high)
    for i in range(PACK):
        row = jnp.where(mine, band[i], other[0, i])
        state[0, i] = row
        state[1, i] = row
        if first:
            power[i] = jnp.where(mine, power_own[i], other[1, i])

    def by_group(value):
        return jnp.where(lane < WIDE, value(0), jnp.where(lane < 2 * WIDE, value(1), value(2)))

    def block(g, i):
        return min(g * PACK + i, BOX - 1) // RB

    advance(
        PACK, True, *work,
        lambda i: by_group(lambda g: base[block(g, i)]),
        lambda m, i: by_group(lambda g: mask[m, block(g, i)]),
        power,
    )
    back = COLS - own_shift(here[1])
    border = ((lane >= COLS - HALO) & left) | ((lane < HALO) & jnp.logical_not(left))
    for r in range(ROWS):
        moved = pltpu.roll(state[0, r % PACK], lax.rem(back + (2 * COLS - (r // PACK) * WIDE), COLS), 1)
        f = jnp.where(border, moved, end[r])
        u = own[r]
        d = decay[r]
        x = native_row(here, r)
        if first:
            offset = f - d * u
            offset_box[r] = offset
            at = lax.div(x, 4) * 8 + lax.rem(x, 4)
            send[pl.ds(at, LAYERS, stride=64), :] = d
            send[pl.ds(at + 4, LAYERS, stride=64), :] = offset
        else:
            du = d * u
            send[pl.ds(x, LAYERS, stride=ROWS), :] = f - du
            jump[pl.ds(x, LAYERS, stride=ROWS), :] = f - (du + offset_before[r])


def border(here, mask, base, end, band, other, own, decay, first, extra):
    if first:
        outs = [plane(PACK), plane(ROWS), jax.ShapeDtypeStruct((512, COLS), jnp.float32)]
    else:
        outs = [jax.ShapeDtypeStruct((256, COLS), jnp.float32)] * 2
    return pl.pallas_call(
        functools.partial(band_kernel, first),
        out_shape=outs,
        in_specs=[sspec(), sspec()] + [spec()] * (6 + len(extra)),
        out_specs=[spec()] * len(outs),
        scratch_shapes=scratch(PACK),
        compiler_params=pltpu.CompilerParams(vmem_limit_bytes=8 * 1024 * 1024),
        name="propagate_band",
    )(here, mask, base, end, band, other, own, decay, *extra)


def cycle_kernel(slabs, rate, offset, out):
    scale = rate(0)
    shift = offset(0)
    for k in range(1, slabs):
        d = rate(k)
        scale = scale * d
        shift = d * shift + offset(k)
    u = shift / (1.0 - scale)
    out[0] = u
    for k in range(slabs - 1):
        u = rate(k) * u + offset(k)
        out[k + 1] = u


def cycle_first(slabs, both, out):
    cycle_kernel(slabs, lambda k: both[k, 0:4], lambda k: both[k, 4:8], out)


def cycle_later(slabs, both, offset, out):
    cycle_kernel(slabs, lambda k: both[k, 0:4], lambda k: offset[k], out)


def cycle(both, offset):
    slabs = both.shape[0]
    args = (both,) if offset is None else (both, offset)
    return pl.pallas_call(
        functools.partial(cycle_first if offset is None else cycle_later, slabs),
        out_shape=jax.ShapeDtypeStruct((slabs, 4, COLS), jnp.float32),
        in_specs=[spec()] * len(args),
        out_specs=spec(),
        compiler_params=pltpu.CompilerParams(vmem_limit_bytes=8 * 1024 * 1024),
        name="cycle",
    )(*args)


def base_rows(region_ids, region_conductivity):
    labels = jnp.arange(REGIONS, dtype=jnp.int32)
    chosen = (region_ids[:, :, None] == labels[None, None, :]).astype(jnp.float32)
    return jnp.sum(chosen * region_conductivity[None, None, :], axis=2)


SWAP = [(0, 1), (1, 0)]


def shards(initial_states, coarse_decay, power_map, power_mask, region_ids, region_conductivity):
    slabs = lax.axis_size("tm")
    sx = lax.axis_index("sx")
    here = jnp.stack([sx, lax.axis_index("sy")]).astype(jnp.int32)
    per_block = base_rows(region_ids, region_conductivity).T
    per_block = jnp.where(sx == 0, per_block, per_block[::-1])
    base = jnp.broadcast_to(per_block[:, :, None], (*per_block.shape, COLS))
    mask = power_mask[0].astype(jnp.float32)
    mask = jnp.where(sx == 0, mask, mask[:, ::-1])
    decay_native = coarse_decay.reshape(LAYERS * ROWS, COLS)

    own, power_own, send = turn(here, [initial_states, power_map])
    halo = lax.ppermute(send, "sx", SWAP)
    sent = pack(here, [own, power_own], halo)
    other = lax.ppermute(sent, "sy", SWAP)
    end, band, power_box, power_band_own, decay = main(
        here, mask, base, own, halo, True, (power_own, decay_native)
    )
    power_band, offset, both = border(
        here, mask, base, end, band, other, own, decay, True, (power_band_own,)
    )
    both = lax.all_to_all(both.reshape(slabs, 8, COLS), "tm", 0, 0, tiled=True)
    states = lax.all_to_all(cycle(both, None), "tm", 0, 0, tiled=True)

    own, send = turn(here, [states])
    halo = lax.ppermute(send, "sx", SWAP)
    sent = pack(here, [own], halo)
    other = lax.ppermute(sent, "sy", SWAP)
    end, band = main(here, mask, base, own, halo, False, (power_box,))
    later, jump = border(
        here, mask, base, end, band, other, own, decay, False, (power_band, offset)
    )
    later = lax.all_to_all(later.reshape(slabs, 4, COLS), "tm", 0, 0, tiled=True)
    states = lax.all_to_all(cycle(both, later), "tm", 0, 0, tiled=True)
    shape = (1, LAYERS, ROWS, COLS)
    return states.reshape(shape), jump.reshape(shape)


def solution(mesh):
    return jax.shard_map(
        shards,
        mesh=mesh,
        in_specs=(
            P("tm", None, "sx", "sy"),
            P("tm", None, "sx", "sy"),
            P(None, "sx", "sy"),
            P("tm", None, None),
            P(),
            P(),
        ),
        out_specs=(P("tm", None, "sx", "sy"), P("tm", None, "sx", "sy")),
        check_vma=False,
    )
```

```python
import functools

import jax
import jax.numpy as jnp
from jax import lax
from jax.experimental import pallas as pl
from jax.experimental.pallas import tpu as pltpu
from jax.sharding import PartitionSpec as P

RB = 8
REGIONS = 4
FSTEPS = 4
SWEEPS = 3
ITERS = 2
cond_slope = 0.25
joule_slope = 0.3

HALO = FSTEPS * SWEEPS
ROWS = 32
LAYERS = 8
COLS = 128
BOX = ROWS + HALO
EDGE = 2 * HALO
WIDE = 64
PACK = 22
BLOCKS = 6
SENT = 9
FRINGE = 8
VMEM = pltpu.VMEM


def spec():
    return pl.BlockSpec(memory_space=VMEM)


def sspec():
    return pl.BlockSpec(memory_space=pltpu.SMEM)


def plane(*shape):
    return jax.ShapeDtypeStruct((*shape, LAYERS, COLS), jnp.float32)


def flat(rows):
    return jax.ShapeDtypeStruct((rows, COLS), jnp.float32)


def call(kernel, outs, scalars, arrays, name, work=(), cost=None, place=VMEM):
    single = not isinstance(outs, list)
    return pl.pallas_call(
        kernel,
        out_shape=outs,
        in_specs=[sspec()] * len(scalars) + [pl.BlockSpec(memory_space=place)] * len(arrays),
        out_specs=spec() if single else [spec()] * len(outs),
        scratch_shapes=list(work),
        cost_estimate=cost,
        compiler_params=pltpu.CompilerParams(vmem_limit_bytes=8 * 1024 * 1024),
        name=name,
    )(*scalars, *arrays)


def lanes():
    return lax.broadcasted_iota(jnp.int32, (LAYERS, COLS), 1)


def layers():
    return lax.broadcasted_iota(jnp.int32, (LAYERS, COLS), 0)


def moved(value, known, unknown=None):
    known = known % COLS
    if unknown is None:
        return pltpu.roll(value, known, 1) if known else value
    return pltpu.roll(value, (unknown + known) & (COLS - 1), 1)


def native_row(here, r):
    return jnp.where(here[0] == 0, r, ROWS - 1 - r)


def native(here, ref, r):
    return ref[pl.ds(native_row(here, r), LAYERS, stride=ROWS), :]


def box_row(here, own, far, r):
    return own[r] if r < ROWS else native(here, far, r - ROWS)


def load_kernel(here, *refs):
    arrays, outs, held, sem = refs[:3], refs[3:6], refs[6], refs[7]
    copies = [pltpu.make_async_copy(arrays[k], held.at[k], sem.at[k]) for k in range(3)]
    for copy in copies:
        copy.start()
    for k in range(3):
        copies[k].wait()
        for r in range(ROWS):
            outs[k][r] = native(here, held.at[k], r)


def banded(i, row):
    return jnp.where(lanes() < WIDE, moved(row(i), EDGE), moved(row(PACK + i), EDGE + WIDE))


class Part:
    def __init__(self, n, packed, power, base, heat, work):
        self.n, self.packed, self.power, self.base, self.heat = n, packed, power, base, heat
        self.state, self.tmp, self.wx, self.wyp, self.wzp, self.inv, self.rhs = work

    def prepare(self, m, now, old, coef_now, coef_old, half):
        n, packed = self.n, self.packed
        lane = lanes()
        layer = layers()
        edge = jnp.where(layer == 0, 1.0, 0.0)
        if not packed:
            edge = edge + jnp.where(lane == 0, 1.0, 0.0) + jnp.where(lane == COLS - 1, 1.0, 0.0)
        cond = []
        for r in range(n):
            cur = self.state[now, r]
            tanh = jnp.tanh(cur)
            cond.append((half * self.base(r)) * (1.0 - cond_slope * tanh))
            source = (half * self.heat(m, r)) * self.power[r] * (1.0 + joule_slope * tanh)
            self.rhs[r] = (coef_now * cur + coef_old * self.state[old, r]) + source
        faces = [None] * (n + 1)
        for r in range(1, n):
            faces[r] = cond[r - 1] + cond[r]
        if packed:
            faces[0] = jnp.where(lane < WIDE, 0.0, cond[0] + moved(cond[n - 1], WIDE))
            faces[n] = cond[n - 1] + moved(cond[0], WIDE)
        for r in range(n):
            c = cond[r]
            north = c + moved(c, -1)
            if not packed:
                north = jnp.where(lane == COLS - 1, 0.0, north)
            up = jnp.where(layer == LAYERS - 1, 0.0, 0.5 * (c + pltpu.roll(c, LAYERS - 1, 0)))
            total = (north + moved(north, 1)) + (up + pltpu.roll(up, 1, 0)) + (1.0 + edge * c)
            low = faces[r]
            if r == 0:
                low = c if low is None else low + jnp.where(lane < WIDE, c, 0.0)
            high = c if faces[r + 1] is None else faces[r + 1]
            self.wyp[r] = north
            self.wzp[r] = up
            self.inv[r] = 1.0 / (total + (low + high))
        for r in range(n + 1):
            if faces[r] is not None:
                self.wx[r] = faces[r]

    def sweep(self, source, store):
        n, packed = self.n, self.packed
        vs = [source(r) for r in range(n)]
        for r in range(n):
            v = vs[r]
            north = self.wyp[r]
            up = self.wzp[r]
            across = north * moved(v, -1) + moved(north * v, 1)
            along = up * pltpu.roll(v, LAYERS - 1, 0) + pltpu.roll(up * v, 1, 0)
            acc = self.rhs[r]
            if r:
                acc = acc + self.wx[r] * vs[r - 1]
            elif packed:
                acc = acc + self.wx[0] * moved(vs[n - 1], WIDE)
            if r < n - 1:
                acc = acc + self.wx[r + 1] * vs[r + 1]
            elif packed:
                acc = acc + self.wx[n] * moved(vs[0], WIDE)
            store(r, (acc + (across + along)) * self.inv[r])

    def relax(self, k, now, old):
        state, tmp = self.state, self.tmp

        def first(r, value):
            tmp[0, r] = value

        def second(r, value):
            tmp[1, r] = value

        def third(r, value):
            state[old, r] = value

        if k == 0:
            self.sweep(lambda r: state[now, r], first)
        elif k == 1:
            self.sweep(lambda r: tmp[0, r], second)
        else:
            self.sweep(lambda r: tmp[1, r], third)


def advance(*parts):
    def step(m, carry):
        start = m == 0
        now = lax.rem(m, 2)
        old = 1 - now
        coef_now = jnp.where(start, 1.0, 4.0 / 3.0).astype(jnp.float32)
        coef_old = jnp.where(start, 0.0, -1.0 / 3.0).astype(jnp.float32)
        half = jnp.where(start, 0.5, 1.0 / 3.0).astype(jnp.float32)
        for part in parts:
            part.prepare(m, now, old, coef_now, coef_old, half)
        for k in range(SWEEPS):
            for part in parts:
                part.relax(k, now, old)
        return carry

    lax.fori_loop(0, FSTEPS, step, 0)


def work_of(n):
    return [VMEM((2, n, LAYERS, COLS), jnp.float32)] * 2 + [VMEM((n + 1, LAYERS, COLS), jnp.float32)] * 5


def turned(here, block):
    return jnp.where(here[0] == 0, block, 7 - block)


def mask_of(here, mask):
    return lambda m, block: mask[m, turned(here, block)].astype(jnp.float32)


def tile_part(here, mask, base, power, work):
    on = mask_of(here, mask)
    return Part(BOX, False, power, lambda r: base[r // RB], lambda m, r: on(m, r // RB), work)


def band_part(here, mask, base, power, work):
    on = mask_of(here, mask)
    low = lanes() < WIDE

    def two(value):
        return lambda i: jnp.where(low, value(i // RB), value((i + PACK) // RB))

    return Part(PACK, True, power, two(lambda b: base[b]), lambda m, i: two(lambda b: on(m, b))(i), work)


def pack_kernel(here, own, far, power_own, power_far, rate, out):
    left = here[1] == 0
    lane = lanes()
    edge = jnp.where(left, EDGE, 0)
    fringe = jnp.where(left, HALO, 0)
    for k, (near, other) in enumerate(((own, far), (power_own, power_far))):
        for i in range(SENT):
            value = None
            for q in range(5):
                r = min(q * SENT + i, BOX - 1)
                part = moved(box_row(here, near, other, r), q * EDGE, edge)
                value = part if value is None else jnp.where(lane < q * EDGE, value, part)
            out[k * SENT + i] = value
    for j in range(FRINGE):
        value = None
        for g in range(4):
            part = moved(rate[g * FRINGE + j], g * 32, fringe)
            value = part if value is None else jnp.where(lane < g * 32, value, part)
        out[2 * SENT + j] = jnp.where((lane & 31) < HALO, value, 0.0)


def tile_kernel(here, mask, ids, conductivity, own, far, power_own, power_far, *refs):
    end, base, power, band, power_band, *work = refs
    state = work[0]
    layer = layers()
    for b in range(BLOCKS):
        value = jnp.zeros((LAYERS, COLS), jnp.float32)
        for l in range(LAYERS):
            value = jnp.where(layer == l, conductivity[ids[l, turned(here, b)]], value)
        base[b] = value
    for r in range(BOX):
        row = box_row(here, own, far, r)
        state[0, r] = row
        state[1, r] = row
        power[r] = box_row(here, power_own, power_far, r)
    for i in range(PACK):
        band[i] = banded(i, lambda r: state[0, r])
        power_band[i] = banded(i, lambda r: power[r])
    advance(tile_part(here, mask, base, power, work))
    for r in range(ROWS):
        end[r] = state[0, r]


def fringe_shift(left):
    return jnp.where(left, EDGE, HALO)


def merged(here, r, state, end):
    lane = lanes()
    left = here[1] == 0
    border = ((lane >= COLS - HALO) & left) | ((lane < HALO) & jnp.logical_not(left))
    return jnp.where(border, moved(state[0, r % PACK], -EDGE - WIDE * (r // PACK)), end)


def band_kernel(here, mask, end, start, rate, base, band, power_own, other, *refs):
    power, offset_out, send, first_band, *work = refs
    state = work[0]
    lane = lanes()
    left = here[1] == 0
    mine = ((lane & (WIDE - 1)) < EDGE) == left
    place = jnp.where(left, EDGE, 0)

    def received(k, i):
        parts = []
        for g in range(2):
            r = g * PACK + i
            parts.append(moved(other[k * SENT + r % SENT], g * WIDE - EDGE * (r // SENT), place))
        return jnp.where(lane < WIDE, parts[0], parts[1])

    for i in range(PACK):
        row = jnp.where(mine, band[i], received(0, i))
        state[0, i] = row
        state[1, i] = row
        first_band[i] = row
        power[i] = jnp.where(mine, power_own[i], received(1, i))
    advance(band_part(here, mask, base, power, work))
    for r in range(ROWS):
        d = rate[r]
        offset = merged(here, r, state, end[r]) - d * start[r]
        offset_out[r] = offset
        x = native_row(here, r)
        at = lax.div(x, 4) * 10 + lax.rem(x, 4)
        send[pl.ds(at, LAYERS, stride=80), :] = d
        send[pl.ds(at + 5, LAYERS, stride=80), :] = offset
    back = COLS - fringe_shift(left)
    for j in range(FRINGE):
        first, last = None, None
        for g in range(4):
            r = g * FRINGE + j
            by = g * 32 - WIDE * (r // PACK)
            u = moved(first_band[r % PACK], by, back)
            f = moved(state[0, r % PACK], by, back)
            first = u if g == 0 else jnp.where(lane < g * 32, first, u)
            last = f if g == 0 else jnp.where(lane < g * 32, last, f)
        d = other[2 * SENT + j]
        send[pl.ds(j * 80 + 4, LAYERS, stride=10), :] = d
        send[pl.ds(j * 80 + 9, LAYERS, stride=10), :] = last - d * first


def turn_kernel(here, states, out, send):
    for r in range(ROWS):
        x = native_row(here, r)
        row = states[pl.ds(lax.div(x, 4) * 5 + lax.rem(x, 4), LAYERS, stride=40), :]
        out[r] = row
        if r >= ROWS - HALO:
            send[r - (ROWS - HALO)] = row
    for j in range(FRINGE):
        row = states[pl.ds(j * 40 + 4, LAYERS, stride=5), :]
        out[ROWS + j] = row
        send[HALO + j] = row


def later_kernel(here, mask, own, far, rate, base, power, power_band, offset_before, *refs):
    send, jump, *work = refs
    tile, band = work[:7], work[7:]
    lane = lanes()
    slot = lane & (WIDE - 1)
    left = here[1] == 0
    shift = fringe_shift(left)
    fringe = (slot >= shift) & (slot < shift + HALO)
    for r in range(BOX):
        row = own[r] if r < ROWS else far[BOX - 1 - r]
        tile[0][0, r] = row
        tile[0][1, r] = row
    for i in range(PACK):
        parts = []
        for g in range(2):
            r = g * PACK + i
            source, k, at = (own, r, ROWS) if r < ROWS else (far, 2 * ROWS - 1 - r, HALO)
            parts.append(moved(source[at + k % FRINGE], g * WIDE - 32 * (k // FRINGE), shift))
        beside = jnp.where(lane < WIDE, parts[0], parts[1])
        row = jnp.where(fringe, beside, banded(i, lambda r: tile[0][0, r]))
        band[0][0, i] = row
        band[0][1, i] = row
    advance(
        tile_part(here, mask, base, power, tile),
        band_part(here, mask, base, power_band, band),
    )
    for r in range(ROWS):
        f = merged(here, r, band[0], tile[0][0, r])
        du = rate[r] * own[r]
        x = native_row(here, r)
        send[pl.ds(x, LAYERS, stride=ROWS), :] = f - du
        jump[pl.ds(x, LAYERS, stride=ROWS), :] = f - (du + offset_before[r])


def solve(slabs, rate, offset, store):
    scale = rate(0)
    shift = offset(0)
    for k in range(1, slabs):
        d = rate(k)
        scale = scale * d
        shift = d * shift + offset(k)
    u = shift / (1.0 - scale)
    store(0, u)
    for k in range(slabs - 1):
        u = rate(k) * u + offset(k)
        store(k + 1, u)


def cycle_kernel(slabs, both, out):
    def store(k, u):
        out[5 * k:5 * k + 5] = u

    solve(slabs, lambda k: both[10 * k:10 * k + 5], lambda k: both[10 * k + 5:10 * k + 10], store)


def cycle_later_kernel(slabs, both, offset, out):
    def store(k, u):
        out[k] = u

    solve(slabs, lambda k: both[10 * k:10 * k + 4], lambda k: offset[k], store)


SWAP = [(0, 1), (1, 0)]


def spread(x, slabs):
    x = x.reshape(slabs, x.shape[0] // slabs, 1, COLS)
    return lax.all_to_all(x, "tm", 0, 0, tiled=True).reshape(-1, COLS)


def shards(initial_states, coarse_decay, power_map, power_mask, region_ids, region_conductivity):
    slabs = lax.axis_size("tm")
    here = jnp.stack([lax.axis_index("sx"), lax.axis_index("sy")]).astype(jnp.int32)
    states, powers, decay = (
        x.reshape(LAYERS * ROWS, COLS) for x in (initial_states, power_map, coarse_decay)
    )
    mask = power_mask[0]

    far = lax.ppermute(states, "sx", SWAP)
    power_far = lax.ppermute(powers, "sx", SWAP)
    start, power_own, rate = call(
        load_kernel,
        [plane(ROWS)] * 3,
        [here],
        [pltpu.with_memory_space_constraint(x, pltpu.HBM) for x in (states, powers, decay)],
        "load",
        [VMEM((3, LAYERS * ROWS, COLS), jnp.float32), pltpu.SemaphoreType.DMA((3,))],
        pl.CostEstimate(flops=2_000_000, bytes_accessed=800_000, transcendentals=0),
        pltpu.HBM,
    )
    sent = call(pack_kernel, plane(2 * SENT + FRINGE), [here], [start, far, power_own, power_far, rate], "pack")
    other = lax.ppermute(sent, "sy", SWAP)
    end, base, power, band, power_band = call(
        tile_kernel,
        [plane(n) for n in (ROWS, BLOCKS, BOX, PACK, PACK)],
        [here, mask, region_ids, region_conductivity],
        [start, far, power_own, power_far],
        "propagate_tile",
        work_of(BOX),
        pl.CostEstimate(flops=20_000_000, bytes_accessed=4_000_000, transcendentals=400_000),
    )
    power_band, offset, both = call(
        band_kernel,
        [plane(PACK), plane(ROWS), flat(640)],
        [here, mask],
        [end, start, rate, base, band, power_band, other],
        "propagate_band",
        [VMEM((PACK, LAYERS, COLS), jnp.float32)] + work_of(PACK),
    )
    both = spread(both, slabs)
    states = spread(call(functools.partial(cycle_kernel, slabs), flat(320), [], [both], "cycle"), slabs)

    own, send = call(turn_kernel, [plane(ROWS + FRINGE), plane(HALO + FRINGE)], [here], [states], "turn")
    far = lax.ppermute(send, "sx", SWAP)
    later, jump = call(
        later_kernel,
        [flat(256), flat(256)],
        [here, mask],
        [own, far, rate, base, power, power_band, offset],
        "propagate_later",
        work_of(BOX) + work_of(PACK),
    )
    later = lax.all_to_all(later.reshape(slabs, 4, COLS), "tm", 0, 0, tiled=True)
    states = call(
        functools.partial(cycle_later_kernel, slabs),
        jax.ShapeDtypeStruct((slabs, 4, COLS), jnp.float32), [], [both, later], "cycle_later",
    )
    states = lax.all_to_all(states, "tm", 0, 0, tiled=True)
    shape = (1, LAYERS, ROWS, COLS)
    return states.reshape(shape), jump.reshape(shape)


def solution(mesh):
    return jax.shard_map(
        shards,
        mesh=mesh,
        in_specs=(
            P("tm", None, "sx", "sy"),
            P("tm", None, "sx", "sy"),
            P(None, "sx", "sy"),
            P("tm", None, None),
            P(),
            P(),
        ),
        out_specs=(P("tm", None, "sx", "sy"), P("tm", None, "sx", "sy")),
        check_vma=False,
    )
```

```python
import functools

import jax
import jax.numpy as jnp
from jax import lax
from jax.experimental import pallas as pl
from jax.experimental.pallas import tpu as pltpu
from jax.sharding import PartitionSpec as P

RB = 8
REGIONS = 4
FSTEPS = 4
SWEEPS = 3
ITERS = 2
cond_slope = 0.25
joule_slope = 0.3

HALO = FSTEPS * SWEEPS
ROWS = 32
LAYERS = 8
COLS = 128
BOX = ROWS + HALO
EDGE = 2 * HALO
WIDE = 64
PACK = 22
BLOCKS = 6
SENT = 9
THIN = 4
FRINGE = 8
VMEM = pltpu.VMEM


def spec():
    return pl.BlockSpec(memory_space=VMEM)


def sspec():
    return pl.BlockSpec(memory_space=pltpu.SMEM)


def plane(*shape):
    return jax.ShapeDtypeStruct((*shape, LAYERS, COLS), jnp.float32)


def flat(rows):
    return jax.ShapeDtypeStruct((rows, COLS), jnp.float32)


def call(kernel, outs, scalars, arrays, name, work=(), cost=None, place=VMEM):
    single = not isinstance(outs, list)
    return pl.pallas_call(
        kernel,
        out_shape=outs,
        in_specs=[sspec()] * len(scalars) + [pl.BlockSpec(memory_space=place)] * len(arrays),
        out_specs=spec() if single else [spec()] * len(outs),
        scratch_shapes=list(work),
        cost_estimate=cost,
        compiler_params=pltpu.CompilerParams(vmem_limit_bytes=8 * 1024 * 1024),
        name=name,
    )(*scalars, *arrays)


def lanes():
    return lax.broadcasted_iota(jnp.int32, (LAYERS, COLS), 1)


def layers():
    return lax.broadcasted_iota(jnp.int32, (LAYERS, COLS), 0)


def moved(value, known, unknown=None):
    known = known % COLS
    if unknown is None:
        return pltpu.roll(value, known, 1) if known else value
    return pltpu.roll(value, (unknown + known) & (COLS - 1), 1)


def position():
    return lax.axis_index("sx"), lax.axis_index("sy")


def native_row(here, r):
    return jnp.where(here[0] == 0, r, ROWS - 1 - r)


def native(here, ref, r):
    return ref[pl.ds(native_row(here, r), LAYERS, stride=ROWS), :]


def place_of(here, r, size):
    up, down = (x // 4 * size + x % 4 for x in (r, ROWS - 1 - r))
    return jnp.where(here[0] == 0, up, down)


def box_row(here, own, far, r):
    return own[r] if r < ROWS else native(here, far, r - ROWS)


def load_kernel(*refs):
    here = position()
    arrays, outs, held, sem = refs[:3], refs[3:6], refs[6], refs[7]
    copies = [pltpu.make_async_copy(arrays[k], held.at[k], sem.at[k]) for k in range(3)]
    for copy in copies:
        copy.start()
    for k in range(3):
        copies[k].wait()
        for r in range(ROWS):
            outs[k][r] = native(here, held.at[k], r)


def banded(i, row):
    return jnp.where(lanes() < WIDE, moved(row(i), EDGE), moved(row(PACK + i), EDGE + WIDE))


class Part:
    def __init__(self, n, packed, power, base, heat, work):
        self.n, self.packed, self.power, self.base, self.heat = n, packed, power, base, heat
        self.state, self.wx, self.wyp, self.wzp, self.inv, self.rhs = work

    def prepare(self, m, now, old, coef_now, coef_old, half):
        n, packed = self.n, self.packed
        lane = lanes()
        layer = layers()
        edge = jnp.where(layer == 0, 1.0, 0.0)
        if not packed:
            edge = edge + jnp.where(lane == 0, 1.0, 0.0) + jnp.where(lane == COLS - 1, 1.0, 0.0)
        cond = []
        for r in range(n):
            cur = self.state[now, r]
            tanh = jnp.tanh(cur)
            cond.append((half * self.base(r)) * (1.0 - cond_slope * tanh))
            source = (half * self.heat(m, r)) * self.power[r] * (1.0 + joule_slope * tanh)
            self.rhs[r] = (coef_now * cur + coef_old * self.state[old, r]) + source
        faces = [None] * (n + 1)
        for r in range(1, n):
            faces[r] = cond[r - 1] + cond[r]
        if packed:
            faces[0] = jnp.where(lane < WIDE, 0.0, cond[0] + moved(cond[n - 1], WIDE))
            faces[n] = cond[n - 1] + moved(cond[0], WIDE)
        for r in range(n):
            c = cond[r]
            north = c + moved(c, -1)
            if not packed:
                north = jnp.where(lane == COLS - 1, 0.0, north)
            up = jnp.where(layer == LAYERS - 1, 0.0, 0.5 * (c + pltpu.roll(c, LAYERS - 1, 0)))
            total = (north + moved(north, 1)) + (up + pltpu.roll(up, 1, 0)) + (1.0 + edge * c)
            low = faces[r]
            if r == 0:
                low = c if low is None else low + jnp.where(lane < WIDE, c, 0.0)
            high = c if faces[r + 1] is None else faces[r + 1]
            self.wyp[r] = north
            self.wzp[r] = up
            self.inv[r] = 1.0 / (total + (low + high))
        for r in range(n + 1):
            if faces[r] is not None:
                self.wx[r] = faces[r]

    def sweep(self, vs):
        n, packed = self.n, self.packed
        out = []
        for r in range(n):
            v = vs[r]
            north = self.wyp[r]
            up = self.wzp[r]
            across = north * moved(v, -1) + moved(north * v, 1)
            along = up * pltpu.roll(v, LAYERS - 1, 0) + pltpu.roll(up * v, 1, 0)
            acc = self.rhs[r]
            if r:
                acc = acc + self.wx[r] * vs[r - 1]
            elif packed:
                acc = acc + self.wx[0] * moved(vs[n - 1], WIDE)
            if r < n - 1:
                acc = acc + self.wx[r + 1] * vs[r + 1]
            elif packed:
                acc = acc + self.wx[n] * moved(vs[0], WIDE)
            out.append((acc + (across + along)) * self.inv[r])
        return out


def advance(*parts):
    def turn(t, carry):
        for now in range(2):
            old = 1 - now
            start = (t == 0) if now == 0 else False
            coef_now = jnp.where(start, 1.0, 4.0 / 3.0).astype(jnp.float32)
            coef_old = jnp.where(start, 0.0, -1.0 / 3.0).astype(jnp.float32)
            half = jnp.where(start, 0.5, 1.0 / 3.0).astype(jnp.float32)
            for part in parts:
                part.prepare(2 * t + now, now, old, coef_now, coef_old, half)
            values = [[part.state[now, r] for r in range(part.n)] for part in parts]
            for k in range(SWEEPS):
                values = [part.sweep(vs) for part, vs in zip(parts, values)]
            for part, vs in zip(parts, values):
                for r in range(part.n):
                    part.state[old, r] = vs[r]
        return carry

    lax.fori_loop(0, FSTEPS // 2, turn, 0)


def work_of(n):
    return [VMEM((2, n, LAYERS, COLS), jnp.float32)] + [VMEM((n + 1, LAYERS, COLS), jnp.float32)] * 5


def turned(here, block):
    return jnp.where(here[0] == 0, block, 7 - block)


def tile_part(base, heat, power, work):
    return Part(BOX, False, power, lambda r: base[r // RB], lambda m, r: heat[m * BLOCKS + r // RB], work)


def band_part(base, heat, power, work):
    low = lanes() < WIDE

    def two(ref, first, i):
        return jnp.where(low, ref[first + i // RB], ref[first + (i + PACK) // RB])

    return Part(PACK, True, power, lambda i: two(base, 0, i), lambda m, i: two(heat, m * BLOCKS, i), work)


def pack_kernel(own, far, power_own, power_far, rate, out):
    here = position()
    left = here[1] == 0
    lane = lanes()
    edge = jnp.where(left, EDGE, 0)
    fringe = jnp.where(left, HALO, 0)
    for k, (near, other) in enumerate(((own, far), (power_own, power_far))):
        for i in range(SENT):
            value = None
            for q in range(5):
                r = min(q * SENT + i, BOX - 1)
                part = moved(box_row(here, near, other, r), q * EDGE, edge)
                value = part if value is None else jnp.where(lane < q * EDGE, value, part)
            out[k * SENT + i] = value
    for i in range(THIN):
        value = None
        for q in range(8):
            part = moved(rate[q * THIN + i], q * 16, fringe)
            value = part if value is None else jnp.where(lane < q * 16, value, part)
        out[2 * SENT + i] = value


def tile_kernel(mask, ids, conductivity, own, far, power_own, power_far, *refs):
    here = position()
    end, base, heat, power, band, power_band, *work = refs
    state = work[0]
    layer = layers()
    for b in range(BLOCKS):
        value = jnp.zeros((LAYERS, COLS), jnp.float32)
        for l in range(LAYERS):
            value = jnp.where(layer == l, conductivity[ids[l, turned(here, b)]], value)
        base[b] = value
        for m in range(FSTEPS):
            on = mask[m, turned(here, b)].astype(jnp.float32)
            heat[m * BLOCKS + b] = jnp.full((LAYERS, COLS), on, jnp.float32)
    for r in range(BOX):
        row = box_row(here, own, far, r)
        state[0, r] = row
        state[1, r] = row
        power[r] = box_row(here, power_own, power_far, r)
    for i in range(PACK):
        band[i] = banded(i, lambda r: state[0, r])
        power_band[i] = banded(i, lambda r: power[r])
    advance(tile_part(base, heat, power, work))
    for r in range(ROWS):
        end[r] = state[0, r]


def fringe_shift(left):
    return jnp.where(left, EDGE, HALO)


def merged(here, r, state, end):
    lane = lanes()
    left = here[1] == 0
    border = ((lane >= COLS - HALO) & left) | ((lane < HALO) & jnp.logical_not(left))
    return jnp.where(border, moved(state[0, r % PACK], -EDGE - WIDE * (r // PACK)), end)


def band_kernel(end, start, rate, base, heat, band, power_own, other, *refs):
    here = position()
    power, offset_out, send, first_band, *work = refs
    state = work[0]
    lane = lanes()
    left = here[1] == 0
    mine = ((lane & (WIDE - 1)) < EDGE) == left
    place = jnp.where(left, EDGE, 0)

    def received(k, i):
        parts = []
        for g in range(2):
            r = g * PACK + i
            parts.append(moved(other[k * SENT + r % SENT], g * WIDE - EDGE * (r // SENT), place))
        return jnp.where(lane < WIDE, parts[0], parts[1])

    for i in range(PACK):
        row = jnp.where(mine, band[i], received(0, i))
        state[0, i] = row
        state[1, i] = row
        first_band[i] = row
        power[i] = jnp.where(mine, power_own[i], received(1, i))
    advance(band_part(base, heat, power, work))
    for r in range(ROWS):
        d = rate[r]
        offset = merged(here, r, state, end[r]) - d * start[r]
        offset_out[r] = offset
        at = place_of(here, r, 10)
        send[pl.ds(at, LAYERS, stride=80), :] = d
        send[pl.ds(at + 5, LAYERS, stride=80), :] = offset
    back = COLS - fringe_shift(left)
    for j in range(FRINGE):
        first, last = None, None
        for g in range(4):
            r = g * FRINGE + j
            by = g * 32 - WIDE * (r // PACK)
            u = moved(first_band[r % PACK], by, back)
            f = moved(state[0, r % PACK], by, back)
            first = u if g == 0 else jnp.where(lane < g * 32, first, u)
            last = f if g == 0 else jnp.where(lane < g * 32, last, f)
        d = moved(other[2 * SENT + j % THIN], -16 * (j // THIN))
        d = jnp.where((lane & 31) < HALO, d, 0.0)
        send[pl.ds(j * 80 + 4, LAYERS, stride=10), :] = d
        send[pl.ds(j * 80 + 9, LAYERS, stride=10), :] = last - d * first


def turn_kernel(states, out, send):
    here = position()
    for r in range(ROWS):
        row = states[pl.ds(place_of(here, r, 5), LAYERS, stride=40), :]
        out[r] = row
        if r >= ROWS - HALO:
            send[r - (ROWS - HALO)] = row
    for j in range(FRINGE):
        row = states[pl.ds(j * 40 + 4, LAYERS, stride=5), :]
        out[ROWS + j] = row
        send[HALO + j] = row


def later_kernel(own, far, rate, base, heat, power, power_band, offset_before, *refs):
    here = position()
    send, jump, *work = refs
    tile, band = work[:6], work[6:]
    lane = lanes()
    slot = lane & (WIDE - 1)
    left = here[1] == 0
    shift = fringe_shift(left)
    fringe = (slot >= shift) & (slot < shift + HALO)
    for r in range(BOX):
        row = own[r] if r < ROWS else far[BOX - 1 - r]
        tile[0][0, r] = row
        tile[0][1, r] = row
    for i in range(PACK):
        parts = []
        for g in range(2):
            r = g * PACK + i
            source, k, at = (own, r, ROWS) if r < ROWS else (far, 2 * ROWS - 1 - r, HALO)
            parts.append(moved(source[at + k % FRINGE], g * WIDE - 32 * (k // FRINGE), shift))
        beside = jnp.where(lane < WIDE, parts[0], parts[1])
        row = jnp.where(fringe, beside, banded(i, lambda r: tile[0][0, r]))
        band[0][0, i] = row
        band[0][1, i] = row
    advance(
        tile_part(base, heat, power, tile),
        band_part(base, heat, power_band, band),
    )
    for r in range(ROWS):
        f = merged(here, r, band[0], tile[0][0, r])
        du = rate[r] * own[r]
        x = native_row(here, r)
        send[pl.ds(x, LAYERS, stride=ROWS), :] = f - du
        jump[pl.ds(x, LAYERS, stride=ROWS), :] = f - (du + offset_before[r])


def solve(slabs, rate, offset, store):
    scale = rate(0)
    shift = offset(0)
    for k in range(1, slabs):
        d = rate(k)
        scale = scale * d
        shift = d * shift + offset(k)
    u = shift / (1.0 - scale)
    store(0, u)
    for k in range(slabs - 1):
        u = rate(k) * u + offset(k)
        store(k + 1, u)


def cycle_kernel(slabs, both, out):
    def store(k, u):
        out[5 * k:5 * k + 5] = u

    solve(slabs, lambda k: both[10 * k:10 * k + 5], lambda k: both[10 * k + 5:10 * k + 10], store)


def cycle_later_kernel(slabs, both, offset, out):
    def store(k, u):
        out[k] = u

    solve(slabs, lambda k: both[10 * k:10 * k + 4], lambda k: offset[k], store)


SWAP = [(0, 1), (1, 0)]


def spread(x, slabs):
    x = x.reshape(slabs, x.shape[0] // slabs, 1, COLS)
    return lax.all_to_all(x, "tm", 0, 0, tiled=True).reshape(-1, COLS)


def shards(initial_states, coarse_decay, power_map, power_mask, region_ids, region_conductivity):
    slabs = lax.axis_size("tm")
    states, powers, decay = (
        x.reshape(LAYERS * ROWS, COLS) for x in (initial_states, power_map, coarse_decay)
    )
    mask = power_mask[0]

    far = lax.ppermute(states, "sx", SWAP)
    power_far = lax.ppermute(powers, "sx", SWAP)
    start, power_own, rate = call(
        load_kernel,
        [plane(ROWS)] * 3,
        [],
        [pltpu.with_memory_space_constraint(x, pltpu.HBM) for x in (states, powers, decay)],
        "load",
        [VMEM((3, LAYERS * ROWS, COLS), jnp.float32), pltpu.SemaphoreType.DMA((3,))],
        pl.CostEstimate(flops=2_000_000, bytes_accessed=800_000, transcendentals=0),
        pltpu.HBM,
    )
    sent = call(pack_kernel, plane(2 * SENT + THIN), [], [start, far, power_own, power_far, rate], "pack")
    other = lax.ppermute(sent, "sy", SWAP)
    end, base, heat, power, band, power_band = call(
        tile_kernel,
        [plane(n) for n in (ROWS, BLOCKS, FSTEPS * BLOCKS, BOX, PACK, PACK)],
        [mask, region_ids, region_conductivity],
        [start, far, power_own, power_far],
        "propagate_tile",
        work_of(BOX),
        pl.CostEstimate(flops=20_000_000, bytes_accessed=4_000_000, transcendentals=400_000),
    )
    power_band, offset, both = call(
        band_kernel,
        [plane(PACK), plane(ROWS), flat(640)],
        [],
        [end, start, rate, base, heat, band, power_band, other],
        "propagate_band",
        [VMEM((PACK, LAYERS, COLS), jnp.float32)] + work_of(PACK),
    )
    both = spread(both, slabs)
    states = spread(call(functools.partial(cycle_kernel, slabs), flat(320), [], [both], "cycle"), slabs)

    own, send = call(turn_kernel, [plane(ROWS + FRINGE), plane(HALO + FRINGE)], [], [states], "turn")
    far = lax.ppermute(send, "sx", SWAP)
    later, jump = call(
        later_kernel,
        [flat(256), flat(256)],
        [],
        [own, far, rate, base, heat, power, power_band, offset],
        "propagate_later",
        work_of(BOX) + work_of(PACK),
    )
    later = lax.all_to_all(later.reshape(slabs, 4, COLS), "tm", 0, 0, tiled=True)
    states = call(
        functools.partial(cycle_later_kernel, slabs),
        jax.ShapeDtypeStruct((slabs, 4, COLS), jnp.float32), [], [both, later], "cycle_later",
    )
    states = lax.all_to_all(states, "tm", 0, 0, tiled=True)
    shape = (1, LAYERS, ROWS, COLS)
    return states.reshape(shape), jump.reshape(shape)


def solution(mesh):
    return jax.shard_map(
        shards,
        mesh=mesh,
        in_specs=(
            P("tm", None, "sx", "sy"),
            P("tm", None, "sx", "sy"),
            P(None, "sx", "sy"),
            P("tm", None, None),
            P(),
            P(),
        ),
        out_specs=(P("tm", None, "sx", "sy"), P("tm", None, "sx", "sy")),
        check_vma=False,
    )
```

```python
import functools

import jax
import jax.numpy as jnp
from jax import lax
from jax.experimental import pallas as pl
from jax.experimental.pallas import tpu as pltpu
from jax.sharding import PartitionSpec as P

RB = 8
REGIONS = 4
FSTEPS = 4
SWEEPS = 3
ITERS = 2
cond_slope = 0.25
joule_slope = 0.3

HALO = FSTEPS * SWEEPS
ROWS = 32
LAYERS = 8
COLS = 128
BOX = ROWS + HALO
EDGE = 2 * HALO
WIDE = 64
PACK = 22
BLOCKS = 6
SENT = 9
THIN = 4
FRINGE = 8
VMEM = pltpu.VMEM


def spec():
    return pl.BlockSpec(memory_space=VMEM)


def sspec():
    return pl.BlockSpec(memory_space=pltpu.SMEM)


def plane(*shape):
    return jax.ShapeDtypeStruct((*shape, LAYERS, COLS), jnp.float32)


def flat(rows):
    return jax.ShapeDtypeStruct((rows, COLS), jnp.float32)


def call(kernel, outs, scalars, arrays, name, work=(), cost=None, place=VMEM):
    single = not isinstance(outs, list)
    return pl.pallas_call(
        kernel,
        out_shape=outs,
        in_specs=[sspec()] * len(scalars) + [pl.BlockSpec(memory_space=place)] * len(arrays),
        out_specs=spec() if single else [spec()] * len(outs),
        scratch_shapes=list(work),
        cost_estimate=cost,
        compiler_params=pltpu.CompilerParams(vmem_limit_bytes=8 * 1024 * 1024),
        name=name,
    )(*scalars, *arrays)


def lanes():
    return lax.broadcasted_iota(jnp.int32, (LAYERS, COLS), 1)


def layers():
    return lax.broadcasted_iota(jnp.int32, (LAYERS, COLS), 0)


def moved(value, known, unknown=None):
    known = known % COLS
    if unknown is None:
        return pltpu.roll(value, known, 1) if known else value
    return pltpu.roll(value, (unknown + known) & (COLS - 1), 1)


def position():
    return lax.axis_index("sx"), lax.axis_index("sy")


def native_row(here, r):
    return jnp.where(here[0] == 0, r, ROWS - 1 - r)


def native(here, ref, r):
    return ref[pl.ds(native_row(here, r), LAYERS, stride=ROWS), :]


def place_of(here, r, size):
    up, down = (x // 4 * size + 1 + x % 4 for x in (r, ROWS - 1 - r))
    return jnp.where(here[0] == 0, up, down)


def box_row(here, own, far, r):
    return own[r] if r < ROWS else native(here, far, r - ROWS)


def load_kernel(*refs):
    here = position()
    arrays, outs, held, sem = refs[:3], refs[3:6], refs[6], refs[7]
    copies = [pltpu.make_async_copy(arrays[k], held.at[k], sem.at[k]) for k in range(3)]
    for copy in copies:
        copy.start()
    for k in range(3):
        copies[k].wait()
        for r in range(ROWS):
            outs[k][r] = native(here, held.at[k], r)


def banded(i, row):
    return jnp.where(lanes() < WIDE, moved(row(i), EDGE), moved(row(PACK + i), EDGE + WIDE))


class Part:
    def __init__(self, n, packed, power, base, heat, work):
        self.n, self.packed, self.power, self.base, self.heat = n, packed, power, base, heat
        self.state, self.wx, self.wyp, self.wzp, self.inv, self.rhs = work

    def prepare(self, m, now, old, coef_now, coef_old, half):
        n, packed = self.n, self.packed
        lane = lanes()
        layer = layers()
        edge = jnp.where(layer == 0, 1.0, 0.0)
        if not packed:
            edge = edge + jnp.where(lane == 0, 1.0, 0.0) + jnp.where(lane == COLS - 1, 1.0, 0.0)
        cond = []
        for r in range(n):
            cur = self.state[now, r]
            tanh = jnp.tanh(cur)
            cond.append((half * self.base(r)) * (1.0 - cond_slope * tanh))
            source = (half * self.heat(m, r)) * self.power[r] * (1.0 + joule_slope * tanh)
            if m:
                self.rhs[r] = (coef_now * cur + coef_old * self.state[old, r]) + source
            else:
                self.rhs[r] = cur + source
        faces = [None] * (n + 1)
        for r in range(1, n):
            faces[r] = cond[r - 1] + cond[r]
        if packed:
            faces[0] = jnp.where(lane < WIDE, 0.0, cond[0] + moved(cond[n - 1], WIDE))
            faces[n] = cond[n - 1] + moved(cond[0], WIDE)
        for r in range(n):
            c = cond[r]
            north = c + moved(c, -1)
            if not packed:
                north = jnp.where(lane == COLS - 1, 0.0, north)
            up = jnp.where(layer == LAYERS - 1, 0.0, 0.5 * (c + pltpu.roll(c, LAYERS - 1, 0)))
            total = (north + moved(north, 1)) + (up + pltpu.roll(up, 1, 0)) + (1.0 + edge * c)
            low = faces[r]
            if r == 0:
                low = c if low is None else low + jnp.where(lane < WIDE, c, 0.0)
            high = c if faces[r + 1] is None else faces[r + 1]
            self.wyp[r] = north
            self.wzp[r] = up
            self.inv[r] = 1.0 / (total + (low + high))
        for r in range(n + 1):
            if faces[r] is not None:
                self.wx[r] = faces[r]

    def sweep(self, vs):
        n, packed = self.n, self.packed
        out = []
        for r in range(n):
            v = vs[r]
            north = self.wyp[r]
            up = self.wzp[r]
            across = north * moved(v, -1) + moved(north * v, 1)
            along = up * pltpu.roll(v, LAYERS - 1, 0) + pltpu.roll(up * v, 1, 0)
            acc = self.rhs[r]
            if r:
                acc = acc + self.wx[r] * vs[r - 1]
            elif packed:
                acc = acc + self.wx[0] * moved(vs[n - 1], WIDE)
            if r < n - 1:
                acc = acc + self.wx[r + 1] * vs[r + 1]
            elif packed:
                acc = acc + self.wx[n] * moved(vs[0], WIDE)
            out.append((acc + (across + along)) * self.inv[r])
        return out


def advance(*parts):
    for m in range(FSTEPS):
        now = m % 2
        old = 1 - now
        coefs = (4.0 / 3.0, -1.0 / 3.0, 1.0 / 3.0) if m else (1.0, 0.0, 0.5)
        for part in parts:
            part.prepare(m, now, old, *coefs)
        values = [[part.state[now, r] for r in range(part.n)] for part in parts]
        for k in range(SWEEPS):
            values = [part.sweep(vs) for part, vs in zip(parts, values)]
        for part, vs in zip(parts, values):
            for r in range(part.n):
                part.state[old, r] = vs[r]


def work_of(n):
    return [VMEM((2, n, LAYERS, COLS), jnp.float32)] + [VMEM((n + 1, LAYERS, COLS), jnp.float32)] * 5


def turned(here, block):
    return jnp.where(here[0] == 0, block, 7 - block)


def tile_part(base, heat, power, work):
    return Part(BOX, False, power, lambda r: base[r // RB], lambda m, r: heat[m * BLOCKS + r // RB], work)


def band_part(base, heat, power, work):
    low = lanes() < WIDE

    def two(ref, first, i):
        return jnp.where(low, ref[first + i // RB], ref[first + (i + PACK) // RB])

    return Part(PACK, True, power, lambda i: two(base, 0, i), lambda m, i: two(heat, m * BLOCKS, i), work)


def pack_kernel(own, far, power_own, power_far, rate, out):
    here = position()
    left = here[1] == 0
    lane = lanes()
    edge = jnp.where(left, EDGE, 0)
    fringe = jnp.where(left, HALO, 0)
    for k, (near, other) in enumerate(((own, far), (power_own, power_far))):
        for i in range(SENT):
            value = None
            for q in range(5):
                r = min(q * SENT + i, BOX - 1)
                part = moved(box_row(here, near, other, r), q * EDGE, edge)
                value = part if value is None else jnp.where(lane < q * EDGE, value, part)
            out[k * SENT + i] = value
    for i in range(THIN):
        value = None
        for q in range(8):
            part = moved(rate[q * THIN + i], q * 16, fringe)
            value = part if value is None else jnp.where(lane < q * 16, value, part)
        out[2 * SENT + i] = value


def tile_kernel(mask, ids, conductivity, own, far, power_own, power_far, *refs):
    here = position()
    end, base, heat, power, band, power_band, *work = refs
    state = work[0]
    layer = layers()
    for b in range(BLOCKS):
        value = jnp.zeros((LAYERS, COLS), jnp.float32)
        for l in range(LAYERS):
            value = jnp.where(layer == l, conductivity[ids[l, turned(here, b)]], value)
        base[b] = value
        for m in range(FSTEPS):
            on = mask[m, turned(here, b)].astype(jnp.float32)
            heat[m * BLOCKS + b] = jnp.full((LAYERS, COLS), on, jnp.float32)
    for r in range(BOX):
        row = box_row(here, own, far, r)
        state[0, r] = row
        state[1, r] = row
        power[r] = box_row(here, power_own, power_far, r)
    for i in range(PACK):
        band[i] = banded(i, lambda r: state[0, r])
        power_band[i] = banded(i, lambda r: power[r])
    advance(tile_part(base, heat, power, work))
    for r in range(ROWS):
        end[r] = state[0, r]


def fringe_shift(left):
    return jnp.where(left, EDGE, HALO)


def merged(here, r, state, end):
    lane = lanes()
    left = here[1] == 0
    border = ((lane >= COLS - HALO) & left) | ((lane < HALO) & jnp.logical_not(left))
    return jnp.where(border, moved(state[0, r % PACK], -EDGE - WIDE * (r // PACK)), end)


def band_kernel(end, start, rate, base, heat, band, power_own, other, *refs):
    here = position()
    power, offset_out, send, first_band, *work = refs
    state = work[0]
    lane = lanes()
    left = here[1] == 0
    mine = ((lane & (WIDE - 1)) < EDGE) == left
    place = jnp.where(left, EDGE, 0)

    def received(k, i):
        parts = []
        for g in range(2):
            r = g * PACK + i
            parts.append(moved(other[k * SENT + r % SENT], g * WIDE - EDGE * (r // SENT), place))
        return jnp.where(lane < WIDE, parts[0], parts[1])

    for i in range(PACK):
        row = jnp.where(mine, band[i], received(0, i))
        state[0, i] = row
        state[1, i] = row
        first_band[i] = row
        power[i] = jnp.where(mine, power_own[i], received(1, i))
    advance(band_part(base, heat, power, work))
    for r in range(ROWS):
        d = rate[r]
        offset = merged(here, r, state, end[r]) - d * start[r]
        offset_out[r] = offset
        at = place_of(here, r, 9)
        send[pl.ds(at, LAYERS, stride=72), :] = d
        send[pl.ds(at + 4, LAYERS, stride=72), :] = offset
    back = COLS - fringe_shift(left)
    for j in range(FRINGE):
        first, last = None, None
        for g in range(4):
            r = g * FRINGE + j
            by = g * 32 - WIDE * (r // PACK)
            u = moved(first_band[r % PACK], by, back)
            f = moved(state[0, r % PACK], by, back)
            first = u if g == 0 else jnp.where(lane < g * 32, first, u)
            last = f if g == 0 else jnp.where(lane < g * 32, last, f)
        d = moved(other[2 * SENT + j % THIN], -16 * (j // THIN))
        send[pl.ds(j * 72, LAYERS, stride=9), :] = jnp.where((lane & 31) < 16, d, moved(last - d * first, 16))


def turn_kernel(states, out, send):
    here = position()
    for r in range(ROWS):
        row = states[pl.ds(place_of(here, r, 5), LAYERS, stride=40), :]
        out[r] = row
        if r >= ROWS - HALO:
            send[r - (ROWS - HALO)] = row
    for j in range(FRINGE):
        row = states[pl.ds(j * 40, LAYERS, stride=5), :]
        out[ROWS + j] = row
        send[HALO + j] = row


def later_kernel(own, far, rate, base, heat, power, power_band, offset_before, *refs):
    here = position()
    send, jump, *work = refs
    tile, band = work[:6], work[6:]
    lane = lanes()
    slot = lane & (WIDE - 1)
    left = here[1] == 0
    shift = fringe_shift(left)
    fringe = (slot >= shift) & (slot < shift + HALO)
    for r in range(BOX):
        row = own[r] if r < ROWS else far[BOX - 1 - r]
        tile[0][0, r] = row
        tile[0][1, r] = row
    for i in range(PACK):
        parts = []
        for g in range(2):
            r = g * PACK + i
            source, k, at = (own, r, ROWS) if r < ROWS else (far, 2 * ROWS - 1 - r, HALO)
            parts.append(moved(source[at + k % FRINGE], g * WIDE - 32 * (k // FRINGE), shift))
        beside = jnp.where(lane < WIDE, parts[0], parts[1])
        row = jnp.where(fringe, beside, banded(i, lambda r: tile[0][0, r]))
        band[0][0, i] = row
        band[0][1, i] = row
    advance(
        tile_part(base, heat, power, tile),
        band_part(base, heat, power_band, band),
    )
    for r in range(ROWS):
        f = merged(here, r, band[0], tile[0][0, r])
        du = rate[r] * own[r]
        x = native_row(here, r)
        send[pl.ds(x, LAYERS, stride=ROWS), :] = f - du
        jump[pl.ds(x, LAYERS, stride=ROWS), :] = f - (du + offset_before[r])


def solve(slabs, rate, offset, store):
    scale = rate(0)
    shift = offset(0)
    for k in range(1, slabs):
        d = rate(k)
        scale = scale * d
        shift = d * shift + offset(k)
    u = shift / (1.0 - scale)
    store(0, u)
    for k in range(slabs - 1):
        u = rate(k) * u + offset(k)
        store(k + 1, u)


def cycle_kernel(slabs, both, out):
    def store(k, u):
        out[5 * k:5 * k + 5] = u

    row = lax.broadcasted_iota(jnp.int32, (5, COLS), 0)
    slot = lax.broadcasted_iota(jnp.int32, (5, COLS), 1) & 31
    empty = (row == 0) & (slot >= HALO)

    def rate(k):
        return jnp.where(empty, 0.0, both[9 * k:9 * k + 5])

    def offset(k):
        return jnp.where(row == 0, moved(both[9 * k:9 * k + 5], -16), both[9 * k + 4:9 * k + 9])

    solve(slabs, rate, offset, store)


def cycle_later_kernel(slabs, both, offset, out):
    def store(k, u):
        out[k] = u

    solve(slabs, lambda k: both[9 * k + 1:9 * k + 5], lambda k: offset[k], store)


SWAP = [(0, 1), (1, 0)]


def spread(x, slabs):
    x = x.reshape(slabs, x.shape[0] // slabs, 1, COLS)
    return lax.all_to_all(x, "tm", 0, 0, tiled=True).reshape(-1, COLS)


def shards(initial_states, coarse_decay, power_map, power_mask, region_ids, region_conductivity):
    slabs = lax.axis_size("tm")
    states, powers, decay = (
        x.reshape(LAYERS * ROWS, COLS) for x in (initial_states, power_map, coarse_decay)
    )
    mask = power_mask[0]

    far = lax.ppermute(states, "sx", SWAP)
    power_far = lax.ppermute(powers, "sx", SWAP)
    start, power_own, rate = call(
        load_kernel,
        [plane(ROWS)] * 3,
        [],
        [pltpu.with_memory_space_constraint(x, pltpu.HBM) for x in (states, powers, decay)],
        "load",
        [VMEM((3, LAYERS * ROWS, COLS), jnp.float32), pltpu.SemaphoreType.DMA((3,))],
        pl.CostEstimate(flops=2_000_000, bytes_accessed=800_000, transcendentals=0),
        pltpu.HBM,
    )
    sent = call(pack_kernel, plane(2 * SENT + THIN), [], [start, far, power_own, power_far, rate], "pack")
    other = lax.ppermute(sent, "sy", SWAP)
    end, base, heat, power, band, power_band = call(
        tile_kernel,
        [plane(n) for n in (ROWS, BLOCKS, FSTEPS * BLOCKS, BOX, PACK, PACK)],
        [mask, region_ids, region_conductivity],
        [start, far, power_own, power_far],
        "propagate_tile",
        work_of(BOX),
        pl.CostEstimate(flops=20_000_000, bytes_accessed=4_000_000, transcendentals=400_000),
    )
    power_band, offset, both = call(
        band_kernel,
        [plane(PACK), plane(ROWS), flat(576)],
        [],
        [end, start, rate, base, heat, band, power_band, other],
        "propagate_band",
        [VMEM((PACK, LAYERS, COLS), jnp.float32)] + work_of(PACK),
    )
    both = spread(both, slabs)
    states = spread(call(functools.partial(cycle_kernel, slabs), flat(320), [], [both], "cycle"), slabs)

    own, send = call(turn_kernel, [plane(ROWS + FRINGE), plane(HALO + FRINGE)], [], [states], "turn")
    far = lax.ppermute(send, "sx", SWAP)
    later, jump = call(
        later_kernel,
        [flat(256), flat(256)],
        [],
        [own, far, rate, base, heat, power, power_band, offset],
        "propagate_later",
        work_of(BOX) + work_of(PACK),
    )
    later = lax.all_to_all(later.reshape(slabs, 4, COLS), "tm", 0, 0, tiled=True)
    states = call(
        functools.partial(cycle_later_kernel, slabs),
        jax.ShapeDtypeStruct((slabs, 4, COLS), jnp.float32), [], [both, later], "cycle_later",
    )
    states = lax.all_to_all(states, "tm", 0, 0, tiled=True)
    shape = (1, LAYERS, ROWS, COLS)
    return states.reshape(shape), jump.reshape(shape)


def solution(mesh):
    return jax.shard_map(
        shards,
        mesh=mesh,
        in_specs=(
            P("tm", None, "sx", "sy"),
            P("tm", None, "sx", "sy"),
            P(None, "sx", "sy"),
            P("tm", None, None),
            P(),
            P(),
        ),
        out_specs=(P("tm", None, "sx", "sy"), P("tm", None, "sx", "sy")),
        check_vma=False,
    )
```

```python
import functools

import jax
import jax.numpy as jnp
from jax import lax
from jax.experimental import pallas as pl
from jax.experimental.pallas import tpu as pltpu
from jax.sharding import PartitionSpec as P

RB = 8
REGIONS = 4
FSTEPS = 4
SWEEPS = 3
ITERS = 2
cond_slope = 0.25
joule_slope = 0.3

HALO = FSTEPS * SWEEPS
ROWS = 32
LAYERS = 8
COLS = 128
BOX = ROWS + HALO
EDGE = 2 * HALO
WIDE = 64
PACK = 22
BLOCKS = 6
SENT = 9
THIN = 4
FRINGE = 8
VMEM = pltpu.VMEM


def spec():
    return pl.BlockSpec(memory_space=VMEM)


def sspec():
    return pl.BlockSpec(memory_space=pltpu.SMEM)


def plane(*shape):
    return jax.ShapeDtypeStruct((*shape, LAYERS, COLS), jnp.float32)


def flat(rows):
    return jax.ShapeDtypeStruct((rows, COLS), jnp.float32)


def call(kernel, outs, scalars, arrays, name, work=(), cost=None, place=VMEM):
    single = not isinstance(outs, list)
    return pl.pallas_call(
        kernel,
        out_shape=outs,
        in_specs=[sspec()] * len(scalars) + [pl.BlockSpec(memory_space=place)] * len(arrays),
        out_specs=spec() if single else [spec()] * len(outs),
        scratch_shapes=list(work),
        cost_estimate=cost,
        compiler_params=pltpu.CompilerParams(vmem_limit_bytes=8 * 1024 * 1024),
        name=name,
    )(*scalars, *arrays)


def lanes():
    return lax.broadcasted_iota(jnp.int32, (LAYERS, COLS), 1)


def layers():
    return lax.broadcasted_iota(jnp.int32, (LAYERS, COLS), 0)


def moved(value, known, unknown=None):
    known = known % COLS
    if unknown is None:
        return pltpu.roll(value, known, 1) if known else value
    return pltpu.roll(value, (unknown + known) & (COLS - 1), 1)


def position():
    return lax.axis_index("sx"), lax.axis_index("sy")


def native_row(here, r):
    return jnp.where(here[0] == 0, r, ROWS - 1 - r)


def native(here, ref, r):
    return ref[pl.ds(native_row(here, r), LAYERS, stride=ROWS), :]


def place_of(here, r, size):
    up, down = (x // 4 * size + 1 + x % 4 for x in (r, ROWS - 1 - r))
    return jnp.where(here[0] == 0, up, down)


def box_row(here, own, far, r):
    return own[r] if r < ROWS else native(here, far, r - ROWS)


def load_kernel(*refs):
    here = position()
    arrays, outs, held, sem = refs[:3], refs[3:6], refs[6], refs[7]
    copies = [pltpu.make_async_copy(arrays[k], held.at[k], sem.at[k]) for k in range(3)]
    for copy in copies:
        copy.start()
    for k in range(3):
        copies[k].wait()
        for r in range(ROWS):
            outs[k][r] = native(here, held.at[k], r)


def banded(i, row):
    return jnp.where(lanes() < WIDE, moved(row(i), EDGE), moved(row(PACK + i), EDGE + WIDE))


class Part:
    def __init__(self, n, packed, power, base, heat, work):
        self.n, self.packed, self.power, self.base, self.heat = n, packed, power, base, heat
        self.state, self.wx, self.wyp, self.wzp, self.inv, self.rhs = work

    def prepare(self, m, now, old, coef_now, coef_old, half):
        n, packed = self.n, self.packed
        lane = lanes()
        layer = layers()
        edge = jnp.where(layer == 0, 1.0, 0.0)
        if not packed:
            edge = edge + jnp.where(lane == 0, 1.0, 0.0) + jnp.where(lane == COLS - 1, 1.0, 0.0)
        cond = []
        for r in range(n):
            cur = self.state[now, r]
            tanh = jnp.tanh(cur)
            cond.append((half * self.base(r)) * (1.0 - cond_slope * tanh))
            source = (half * self.heat(m, r)) * self.power[r] * (1.0 + joule_slope * tanh)
            if m:
                self.rhs[r] = (coef_now * cur + coef_old * self.state[old, r]) + source
            else:
                self.rhs[r] = cur + source
        faces = [None] * (n + 1)
        for r in range(1, n):
            faces[r] = cond[r - 1] + cond[r]
        if packed:
            faces[0] = jnp.where(lane < WIDE, 0.0, cond[0] + moved(cond[n - 1], WIDE))
            faces[n] = cond[n - 1] + moved(cond[0], WIDE)
        for r in range(n):
            c = cond[r]
            north = c + moved(c, -1)
            if not packed:
                north = jnp.where(lane == COLS - 1, 0.0, north)
            up = jnp.where(layer == LAYERS - 1, 0.0, 0.5 * (c + pltpu.roll(c, LAYERS - 1, 0)))
            total = (north + moved(north, 1)) + (up + pltpu.roll(up, 1, 0)) + (1.0 + edge * c)
            low = faces[r]
            if r == 0:
                low = c if low is None else low + jnp.where(lane < WIDE, c, 0.0)
            high = c if faces[r + 1] is None else faces[r + 1]
            self.wyp[r] = north
            self.wzp[r] = up
            self.inv[r] = 1.0 / (total + (low + high))
        for r in range(n + 1):
            if faces[r] is not None:
                self.wx[r] = faces[r]

    def sweep(self, vs):
        n, packed = self.n, self.packed
        out = []
        for r in range(n):
            v = vs[r]
            north = self.wyp[r]
            up = self.wzp[r]
            across = north * moved(v, -1) + moved(north * v, 1)
            along = up * pltpu.roll(v, LAYERS - 1, 0) + pltpu.roll(up * v, 1, 0)
            acc = self.rhs[r]
            if r:
                acc = acc + self.wx[r] * vs[r - 1]
            elif packed:
                acc = acc + self.wx[0] * moved(vs[n - 1], WIDE)
            if r < n - 1:
                acc = acc + self.wx[r + 1] * vs[r + 1]
            elif packed:
                acc = acc + self.wx[n] * moved(vs[0], WIDE)
            out.append((acc + (across + along)) * self.inv[r])
        return out


def advance(*parts):
    for m in range(FSTEPS):
        now = m % 2
        old = 1 - now
        coefs = (4.0 / 3.0, -1.0 / 3.0, 1.0 / 3.0) if m else (1.0, 0.0, 0.5)
        for part in parts:
            part.prepare(m, now, old, *coefs)
        values = [[part.state[now, r] for r in range(part.n)] for part in parts]
        for k in range(SWEEPS):
            values = [part.sweep(vs) for part, vs in zip(parts, values)]
        for part, vs in zip(parts, values):
            for r in range(part.n):
                part.state[old, r] = vs[r]


def work_of(n):
    return [VMEM((2, n, LAYERS, COLS), jnp.float32)] + [VMEM((n + 1, LAYERS, COLS), jnp.float32)] * 5


def turned(here, block):
    return jnp.where(here[0] == 0, block, 7 - block)


def tile_part(base, heat, power, work):
    return Part(BOX, False, power, lambda r: base[r // RB], lambda m, r: heat[m * BLOCKS + r // RB], work)


def band_part(base, heat, power, work):
    low = lanes() < WIDE

    def two(ref, first, i):
        return jnp.where(low, ref[first + i // RB], ref[first + (i + PACK) // RB])

    return Part(PACK, True, power, lambda i: two(base, 0, i), lambda m, i: two(heat, m * BLOCKS, i), work)


def pack_kernel(own, far, power_own, power_far, rate, out):
    here = position()
    left = here[1] == 0
    lane = lanes()
    edge = jnp.where(left, EDGE, 0)
    fringe = jnp.where(left, HALO, 0)
    for k, (near, other) in enumerate(((own, far), (power_own, power_far))):
        for i in range(SENT):
            value = None
            for q in range(5):
                r = min(q * SENT + i, BOX - 1)
                part = moved(box_row(here, near, other, r), q * EDGE, edge)
                value = part if value is None else jnp.where(lane < q * EDGE, value, part)
            out[k * SENT + i] = value
    for i in range(THIN):
        value = None
        for q in range(8):
            part = moved(rate[q * THIN + i], q * 16, fringe)
            value = part if value is None else jnp.where(lane < q * 16, value, part)
        out[2 * SENT + i] = value


def tile_kernel(mask, ids, conductivity, own, far, power_own, power_far, *refs):
    here = position()
    end, base, heat, power, band, power_band, *work = refs
    state = work[0]
    layer = layers()
    for b in range(BLOCKS):
        value = jnp.zeros((LAYERS, COLS), jnp.float32)
        for l in range(LAYERS):
            value = jnp.where(layer == l, conductivity[ids[l, turned(here, b)]], value)
        base[b] = value
        for m in range(FSTEPS):
            on = mask[m, turned(here, b)].astype(jnp.float32)
            heat[m * BLOCKS + b] = jnp.full((LAYERS, COLS), on, jnp.float32)
    for r in range(BOX):
        row = box_row(here, own, far, r)
        state[0, r] = row
        state[1, r] = row
        power[r] = box_row(here, power_own, power_far, r)
    for i in range(PACK):
        band[i] = banded(i, lambda r: state[0, r])
        power_band[i] = banded(i, lambda r: power[r])
    advance(tile_part(base, heat, power, work))
    for r in range(ROWS):
        end[r] = state[0, r]


def fringe_shift(left):
    return jnp.where(left, EDGE, HALO)


def merged(here, r, state, end):
    lane = lanes()
    left = here[1] == 0
    border = ((lane >= COLS - HALO) & left) | ((lane < HALO) & jnp.logical_not(left))
    return jnp.where(border, moved(state[0, r % PACK], -EDGE - WIDE * (r // PACK)), end)


def band_kernel(end, start, rate, base, heat, band, power_own, other, *refs):
    here = position()
    power, offset_out, send, first_band, *work = refs
    state = work[0]
    lane = lanes()
    left = here[1] == 0
    mine = ((lane & (WIDE - 1)) < EDGE) == left
    place = jnp.where(left, EDGE, 0)

    def received(k, i):
        parts = []
        for g in range(2):
            r = g * PACK + i
            parts.append(moved(other[k * SENT + r % SENT], g * WIDE - EDGE * (r // SENT), place))
        return jnp.where(lane < WIDE, parts[0], parts[1])

    for i in range(PACK):
        row = jnp.where(mine, band[i], received(0, i))
        state[0, i] = row
        state[1, i] = row
        first_band[i] = row
        power[i] = jnp.where(mine, power_own[i], received(1, i))
    advance(band_part(base, heat, power, work))
    for r in range(ROWS):
        d = rate[r]
        offset = merged(here, r, state, end[r]) - d * start[r]
        offset_out[r] = offset
        at = place_of(here, r, 9)
        send[pl.ds(at, LAYERS, stride=72), :] = d
        send[pl.ds(at + 4, LAYERS, stride=72), :] = offset
    back = COLS - fringe_shift(left)
    for j in range(FRINGE):
        first, last = None, None
        for g in range(4):
            r = g * FRINGE + j
            by = g * 32 - WIDE * (r // PACK)
            u = moved(first_band[r % PACK], by, back)
            f = moved(state[0, r % PACK], by, back)
            first = u if g == 0 else jnp.where(lane < g * 32, first, u)
            last = f if g == 0 else jnp.where(lane < g * 32, last, f)
        d = moved(other[2 * SENT + j % THIN], -16 * (j // THIN))
        send[pl.ds(j * 72, LAYERS, stride=9), :] = jnp.where((lane & 31) < 16, d, moved(last - d * first, 16))


def turn_kernel(states, out, send):
    here = position()
    for r in range(ROWS):
        row = states[pl.ds(place_of(here, r, 5), LAYERS, stride=40), :]
        out[r] = row
        if r >= ROWS - HALO:
            send[r - (ROWS - HALO)] = row
    for j in range(FRINGE):
        row = states[pl.ds(j * 40, LAYERS, stride=5), :]
        out[ROWS + j] = row
        send[HALO + j] = row


def later_kernel(own, far, rate, base, heat, power, power_band, offset_before, *refs):
    here = position()
    send, jump, *work = refs
    tile, band = work[:6], work[6:]
    lane = lanes()
    slot = lane & (WIDE - 1)
    left = here[1] == 0
    shift = fringe_shift(left)
    fringe = (slot >= shift) & (slot < shift + HALO)
    for r in range(BOX):
        row = own[r] if r < ROWS else far[BOX - 1 - r]
        tile[0][0, r] = row
        tile[0][1, r] = row
    for i in range(PACK):
        parts = []
        for g in range(2):
            r = g * PACK + i
            source, k, at = (own, r, ROWS) if r < ROWS else (far, 2 * ROWS - 1 - r, HALO)
            parts.append(moved(source[at + k % FRINGE], g * WIDE - 32 * (k // FRINGE), shift))
        beside = jnp.where(lane < WIDE, parts[0], parts[1])
        row = jnp.where(fringe, beside, banded(i, lambda r: tile[0][0, r]))
        band[0][0, i] = row
        band[0][1, i] = row
    advance(
        tile_part(base, heat, power, tile),
        band_part(base, heat, power_band, band),
    )
    for r in range(ROWS):
        f = merged(here, r, band[0], tile[0][0, r])
        du = rate[r] * own[r]
        x = native_row(here, r)
        send[pl.ds(x, LAYERS, stride=ROWS), :] = f - du
        jump[pl.ds(x, LAYERS, stride=ROWS), :] = f - (du + offset_before[r])


def solve(slabs, rate, offset, store):
    scale = rate(0)
    shift = offset(0)
    for k in range(1, slabs):
        d = rate(k)
        scale = scale * d
        shift = d * shift + offset(k)
    u = shift / (1.0 - scale)
    store(0, u)
    for k in range(slabs - 1):
        u = rate(k) * u + offset(k)
        store(k + 1, u)


def cycle_kernel(slabs, both, out):
    def store(k, u):
        out[5 * k:5 * k + 5] = u

    row = lax.broadcasted_iota(jnp.int32, (5, COLS), 0)
    slot = lax.broadcasted_iota(jnp.int32, (5, COLS), 1) & 31
    empty = (row == 0) & (slot >= HALO)

    def rate(k):
        return jnp.where(empty, 0.0, both[9 * k:9 * k + 5])

    def offset(k):
        return jnp.where(row == 0, moved(both[9 * k:9 * k + 5], -16), both[9 * k + 4:9 * k + 9])

    solve(slabs, rate, offset, store)


def cycle_later_kernel(slabs, both, offset, jump, out, jump_out, sem):
    copy = pltpu.make_async_copy(jump, jump_out, sem)
    copy.start()

    def store(k, u):
        out[k] = u

    solve(slabs, lambda k: both[9 * k + 1:9 * k + 5], lambda k: offset[k], store)
    copy.wait()


SWAP = [(0, 1), (1, 0)]


def spread(x, slabs):
    x = x.reshape(slabs, x.shape[0] // slabs, 1, COLS)
    return lax.all_to_all(x, "tm", 0, 0, tiled=True).reshape(-1, COLS)


def shards(initial_states, coarse_decay, power_map, power_mask, region_ids, region_conductivity):
    slabs = lax.axis_size("tm")
    states, powers, decay = (
        x.reshape(LAYERS * ROWS, COLS) for x in (initial_states, power_map, coarse_decay)
    )
    mask = power_mask[0]

    far = lax.ppermute(states, "sx", SWAP)
    power_far = lax.ppermute(powers, "sx", SWAP)
    start, power_own, rate = call(
        load_kernel,
        [plane(ROWS)] * 3,
        [],
        [pltpu.with_memory_space_constraint(x, pltpu.HBM) for x in (states, powers, decay)],
        "load",
        [VMEM((3, LAYERS * ROWS, COLS), jnp.float32), pltpu.SemaphoreType.DMA((3,))],
        pl.CostEstimate(flops=2_000_000, bytes_accessed=800_000, transcendentals=0),
        pltpu.HBM,
    )
    sent = call(pack_kernel, plane(2 * SENT + THIN), [], [start, far, power_own, power_far, rate], "pack")
    other = lax.ppermute(sent, "sy", SWAP)
    end, base, heat, power, band, power_band = call(
        tile_kernel,
        [plane(n) for n in (ROWS, BLOCKS, FSTEPS * BLOCKS, BOX, PACK, PACK)],
        [mask, region_ids, region_conductivity],
        [start, far, power_own, power_far],
        "propagate_tile",
        work_of(BOX),
        pl.CostEstimate(flops=20_000_000, bytes_accessed=4_000_000, transcendentals=400_000),
    )
    power_band, offset, both = call(
        band_kernel,
        [plane(PACK), plane(ROWS), flat(576)],
        [],
        [end, start, rate, base, heat, band, power_band, other],
        "propagate_band",
        [VMEM((PACK, LAYERS, COLS), jnp.float32)] + work_of(PACK),
    )
    both = spread(both, slabs)
    states = spread(call(functools.partial(cycle_kernel, slabs), flat(320), [], [both], "cycle"), slabs)

    own, send = call(turn_kernel, [plane(ROWS + FRINGE), plane(HALO + FRINGE)], [], [states], "turn")
    far = lax.ppermute(send, "sx", SWAP)
    later, jump = call(
        later_kernel,
        [flat(256), flat(256)],
        [],
        [own, far, rate, base, heat, power, power_band, offset],
        "propagate_later",
        work_of(BOX) + work_of(PACK),
    )
    later = lax.all_to_all(later.reshape(slabs, 4, COLS), "tm", 0, 0, tiled=True)
    states, jump = pl.pallas_call(
        functools.partial(cycle_later_kernel, slabs),
        out_shape=[jax.ShapeDtypeStruct((slabs, 4, COLS), jnp.float32), flat(LAYERS * ROWS)],
        in_specs=[spec()] * 3,
        out_specs=[spec(), pl.BlockSpec(memory_space=pl.ANY)],
        scratch_shapes=[pltpu.SemaphoreType.DMA],
        compiler_params=pltpu.CompilerParams(vmem_limit_bytes=8 * 1024 * 1024),
        name="cycle_later",
    )(both, later, jump)
    states = lax.all_to_all(states, "tm", 0, 0, tiled=True)
    shape = (1, LAYERS, ROWS, COLS)
    return states.reshape(shape), jump.reshape(shape)


def solution(mesh):
    return jax.shard_map(
        shards,
        mesh=mesh,
        in_specs=(
            P("tm", None, "sx", "sy"),
            P("tm", None, "sx", "sy"),
            P(None, "sx", "sy"),
            P("tm", None, None),
            P(),
            P(),
        ),
        out_specs=(P("tm", None, "sx", "sy"), P("tm", None, "sx", "sy")),
        check_vma=False,
    )
```

```python
import functools

import jax
import jax.numpy as jnp
from jax import lax
from jax.experimental import pallas as pl
from jax.experimental.pallas import tpu as pltpu
from jax.sharding import PartitionSpec as P

RB = 8
REGIONS = 4
FSTEPS = 4
SWEEPS = 3
ITERS = 2
cond_slope = 0.25
joule_slope = 0.3

HALO = FSTEPS * SWEEPS
ROWS = 32
LAYERS = 8
COLS = 128
BOX = ROWS + HALO
EDGE = 2 * HALO
WIDE = 64
PACK = 22
BLOCKS = 6
SENT = 9
THIN = 4
FRINGE = 8
VMEM = pltpu.VMEM


def spec():
    return pl.BlockSpec(memory_space=VMEM)


def sspec():
    return pl.BlockSpec(memory_space=pltpu.SMEM)


def plane(*shape):
    return jax.ShapeDtypeStruct((*shape, LAYERS, COLS), jnp.float32)


def flat(rows):
    return jax.ShapeDtypeStruct((rows, COLS), jnp.float32)


def call(kernel, outs, scalars, arrays, name, work=(), cost=None, place=VMEM):
    single = not isinstance(outs, list)
    return pl.pallas_call(
        kernel,
        out_shape=outs,
        in_specs=[sspec()] * len(scalars) + [pl.BlockSpec(memory_space=place)] * len(arrays),
        out_specs=spec() if single else [spec()] * len(outs),
        scratch_shapes=list(work),
        cost_estimate=cost,
        compiler_params=pltpu.CompilerParams(vmem_limit_bytes=8 * 1024 * 1024),
        name=name,
    )(*scalars, *arrays)


def lanes():
    return lax.broadcasted_iota(jnp.int32, (LAYERS, COLS), 1)


def layers():
    return lax.broadcasted_iota(jnp.int32, (LAYERS, COLS), 0)


def moved(value, known, unknown=None):
    known = known % COLS
    if unknown is None:
        return pltpu.roll(value, known, 1) if known else value
    return pltpu.roll(value, (unknown + known) & (COLS - 1), 1)


def position():
    return lax.axis_index("sx"), lax.axis_index("sy")


def native_row(here, r):
    return jnp.where(here[0] == 0, r, ROWS - 1 - r)


def native(here, ref, r):
    return ref[pl.ds(native_row(here, r), LAYERS, stride=ROWS), :]


def place_of(here, r, size):
    up, down = (x // 4 * size + 1 + x % 4 for x in (r, ROWS - 1 - r))
    return jnp.where(here[0] == 0, up, down)


def box_row(here, own, far, r):
    return own[r] if r < ROWS else native(here, far, r - ROWS)


def load_kernel(*refs):
    here = position()
    arrays, outs, held, sem = refs[:3], refs[3:6], refs[6], refs[7]
    copies = [pltpu.make_async_copy(arrays[k], held.at[k], sem.at[k]) for k in range(3)]
    for copy in copies:
        copy.start()
    for k in range(3):
        copies[k].wait()
        for r in range(ROWS):
            outs[k][r] = native(here, held.at[k], r)


def banded(i, row):
    return jnp.where(lanes() < WIDE, moved(row(i), EDGE), moved(row(PACK + i), EDGE + WIDE))


class Part:
    def __init__(self, n, packed, power, base, heat, work):
        self.n, self.packed, self.power, self.base, self.heat = n, packed, power, base, heat
        self.state, self.wx, self.wyp, self.wzp, self.inv, self.rhs = work

    def prepare(self, m, now, old, coef_now, coef_old, half):
        n, packed = self.n, self.packed
        lane = lanes()
        layer = layers()
        edge = jnp.where(layer == 0, 1.0, 0.0)
        if not packed:
            edge = edge + jnp.where(lane == 0, 1.0, 0.0) + jnp.where(lane == COLS - 1, 1.0, 0.0)
        cond = []
        for r in range(n):
            cur = self.state[now, r]
            tanh = jnp.tanh(cur)
            cond.append((half * self.base(r)) * (1.0 - cond_slope * tanh))
            source = (half * self.heat(m, r)) * self.power[r] * (1.0 + joule_slope * tanh)
            if m:
                self.rhs[r] = (coef_now * cur + coef_old * self.state[old, r]) + source
            else:
                self.rhs[r] = cur + source
        faces = [None] * (n + 1)
        for r in range(1, n):
            faces[r] = cond[r - 1] + cond[r]
        if packed:
            faces[0] = jnp.where(lane < WIDE, 0.0, cond[0] + moved(cond[n - 1], WIDE))
            faces[n] = cond[n - 1] + moved(cond[0], WIDE)
        for r in range(n):
            c = cond[r]
            north = c + moved(c, -1)
            if not packed:
                north = jnp.where(lane == COLS - 1, 0.0, north)
            up = jnp.where(layer == LAYERS - 1, 0.0, 0.5 * (c + pltpu.roll(c, LAYERS - 1, 0)))
            total = (north + moved(north, 1)) + (up + pltpu.roll(up, 1, 0)) + (1.0 + edge * c)
            low = faces[r]
            if r == 0:
                low = c if low is None else low + jnp.where(lane < WIDE, c, 0.0)
            high = c if faces[r + 1] is None else faces[r + 1]
            self.wyp[r] = north
            self.wzp[r] = up
            self.inv[r] = 1.0 / (total + (low + high))
        for r in range(n + 1):
            if faces[r] is not None:
                self.wx[r] = faces[r]

    def sweep(self, vs):
        n, packed = self.n, self.packed
        out = []
        for r in range(n):
            v = vs[r]
            north = self.wyp[r]
            up = self.wzp[r]
            across = north * moved(v, -1) + moved(north * v, 1)
            along = up * pltpu.roll(v, LAYERS - 1, 0) + pltpu.roll(up * v, 1, 0)
            acc = self.rhs[r]
            if r:
                acc = acc + self.wx[r] * vs[r - 1]
            elif packed:
                acc = acc + self.wx[0] * moved(vs[n - 1], WIDE)
            if r < n - 1:
                acc = acc + self.wx[r + 1] * vs[r + 1]
            elif packed:
                acc = acc + self.wx[n] * moved(vs[0], WIDE)
            out.append((acc + (across + along)) * self.inv[r])
        return out


def advance(*parts):
    for m in range(FSTEPS):
        now = m % 2
        old = 1 - now
        coefs = (4.0 / 3.0, -1.0 / 3.0, 1.0 / 3.0) if m else (1.0, 0.0, 0.5)
        for part in parts:
            part.prepare(m, now, old, *coefs)
        values = [[part.state[now, r] for r in range(part.n)] for part in parts]
        for k in range(SWEEPS):
            values = [part.sweep(vs) for part, vs in zip(parts, values)]
        for part, vs in zip(parts, values):
            for r in range(part.n):
                part.state[old, r] = vs[r]


def work_of(n):
    return [VMEM((2, n, LAYERS, COLS), jnp.float32)] + [VMEM((n + 1, LAYERS, COLS), jnp.float32)] * 5


def turned(here, block):
    return jnp.where(here[0] == 0, block, 7 - block)


def tile_part(base, heat, power, work):
    return Part(BOX, False, power, lambda r: base[r // RB], lambda m, r: heat[m * BLOCKS + r // RB], work)


def band_part(base, heat, power, work):
    low = lanes() < WIDE

    def two(ref, first, i):
        return jnp.where(low, ref[first + i // RB], ref[first + (i + PACK) // RB])

    return Part(PACK, True, power, lambda i: two(base, 0, i), lambda m, i: two(heat, m * BLOCKS, i), work)


def pack_kernel(own, far, power_own, power_far, rate, out):
    here = position()
    left = here[1] == 0
    lane = lanes()
    edge = jnp.where(left, EDGE, 0)
    fringe = jnp.where(left, HALO, 0)
    for k, (near, other) in enumerate(((own, far), (power_own, power_far))):
        for i in range(SENT):
            value = None
            for q in range(5):
                r = min(q * SENT + i, BOX - 1)
                part = moved(box_row(here, near, other, r), q * EDGE, edge)
                value = part if value is None else jnp.where(lane < q * EDGE, value, part)
            out[k * SENT + i] = value
    for i in range(THIN):
        value = None
        for q in range(8):
            part = moved(rate[q * THIN + i], q * 16, fringe)
            value = part if value is None else jnp.where(lane < q * 16, value, part)
        out[2 * SENT + i] = value


def tile_kernel(mask, ids, conductivity, own, far, power_own, power_far, *refs):
    here = position()
    end, base, heat, power, band, power_band, *work = refs
    state = work[0]
    layer = layers()
    for b in range(BLOCKS):
        value = jnp.zeros((LAYERS, COLS), jnp.float32)
        for l in range(LAYERS):
            value = jnp.where(layer == l, conductivity[ids[l, turned(here, b)]], value)
        base[b] = value
        for m in range(FSTEPS):
            on = mask[m, turned(here, b)].astype(jnp.float32)
            heat[m * BLOCKS + b] = jnp.full((LAYERS, COLS), on, jnp.float32)
    for r in range(BOX):
        row = box_row(here, own, far, r)
        state[0, r] = row
        power[r] = box_row(here, power_own, power_far, r)
    for i in range(PACK):
        band[i] = banded(i, lambda r: state[0, r])
        power_band[i] = banded(i, lambda r: power[r])
    advance(tile_part(base, heat, power, work))
    for r in range(ROWS):
        end[r] = state[0, r]


def fringe_shift(left):
    return jnp.where(left, EDGE, HALO)


def merged(here, r, state, end):
    lane = lanes()
    left = here[1] == 0
    border = ((lane >= COLS - HALO) & left) | ((lane < HALO) & jnp.logical_not(left))
    return jnp.where(border, moved(state[0, r % PACK], -EDGE - WIDE * (r // PACK)), end)


def band_kernel(end, start, rate, base, heat, band, power_own, other, *refs):
    here = position()
    power, offset_out, send, first_band, *work = refs
    state = work[0]
    lane = lanes()
    left = here[1] == 0
    mine = ((lane & (WIDE - 1)) < EDGE) == left
    place = jnp.where(left, EDGE, 0)

    def received(k, i):
        parts = []
        for g in range(2):
            r = g * PACK + i
            parts.append(moved(other[k * SENT + r % SENT], g * WIDE - EDGE * (r // SENT), place))
        return jnp.where(lane < WIDE, parts[0], parts[1])

    for i in range(PACK):
        row = jnp.where(mine, band[i], received(0, i))
        state[0, i] = row
        first_band[i] = row
        power[i] = jnp.where(mine, power_own[i], received(1, i))
    advance(band_part(base, heat, power, work))
    for r in range(ROWS):
        d = rate[r]
        offset = merged(here, r, state, end[r]) - d * start[r]
        offset_out[r] = offset
        at = place_of(here, r, 9)
        send[pl.ds(at, LAYERS, stride=72), :] = d
        send[pl.ds(at + 4, LAYERS, stride=72), :] = offset
    back = COLS - fringe_shift(left)
    for j in range(FRINGE):
        first, last = None, None
        for g in range(4):
            r = g * FRINGE + j
            by = g * 32 - WIDE * (r // PACK)
            u = moved(first_band[r % PACK], by, back)
            f = moved(state[0, r % PACK], by, back)
            first = u if g == 0 else jnp.where(lane < g * 32, first, u)
            last = f if g == 0 else jnp.where(lane < g * 32, last, f)
        d = moved(other[2 * SENT + j % THIN], -16 * (j // THIN))
        send[pl.ds(j * 72, LAYERS, stride=9), :] = jnp.where((lane & 31) < 16, d, moved(last - d * first, 16))


def turn_kernel(states, out, send):
    here = position()
    for r in range(ROWS):
        row = states[pl.ds(place_of(here, r, 5), LAYERS, stride=40), :]
        out[r] = row
        if r >= ROWS - HALO:
            send[r - (ROWS - HALO)] = row
    for j in range(FRINGE):
        row = states[pl.ds(j * 40, LAYERS, stride=5), :]
        out[ROWS + j] = row
        send[HALO + j] = row


def later_kernel(own, far, rate, base, heat, power, power_band, offset_before, *refs):
    here = position()
    send, jump, *work = refs
    tile, band = work[:6], work[6:]
    lane = lanes()
    slot = lane & (WIDE - 1)
    left = here[1] == 0
    shift = fringe_shift(left)
    fringe = (slot >= shift) & (slot < shift + HALO)
    for r in range(BOX):
        row = own[r] if r < ROWS else far[BOX - 1 - r]
        tile[0][0, r] = row
    for i in range(PACK):
        parts = []
        for g in range(2):
            r = g * PACK + i
            source, k, at = (own, r, ROWS) if r < ROWS else (far, 2 * ROWS - 1 - r, HALO)
            parts.append(moved(source[at + k % FRINGE], g * WIDE - 32 * (k // FRINGE), shift))
        beside = jnp.where(lane < WIDE, parts[0], parts[1])
        row = jnp.where(fringe, beside, banded(i, lambda r: tile[0][0, r]))
        band[0][0, i] = row
    advance(
        tile_part(base, heat, power, tile),
        band_part(base, heat, power_band, band),
    )
    for r in range(ROWS):
        f = merged(here, r, band[0], tile[0][0, r])
        du = rate[r] * own[r]
        x = native_row(here, r)
        send[pl.ds(x, LAYERS, stride=ROWS), :] = f - du
        jump[pl.ds(x, LAYERS, stride=ROWS), :] = f - (du + offset_before[r])


def solve(slabs, rate, offset, store):
    scale = rate(0)
    shift = offset(0)
    for k in range(1, slabs):
        d = rate(k)
        scale = scale * d
        shift = d * shift + offset(k)
    u = shift / (1.0 - scale)
    store(0, u)
    for k in range(slabs - 1):
        u = rate(k) * u + offset(k)
        store(k + 1, u)


def cycle_kernel(slabs, both, out):
    def store(k, u):
        out[5 * k:5 * k + 5] = u

    row = lax.broadcasted_iota(jnp.int32, (5, COLS), 0)
    slot = lax.broadcasted_iota(jnp.int32, (5, COLS), 1) & 31
    empty = (row == 0) & (slot >= HALO)

    def rate(k):
        return jnp.where(empty, 0.0, both[9 * k:9 * k + 5])

    def offset(k):
        return jnp.where(row == 0, moved(both[9 * k:9 * k + 5], -16), both[9 * k + 4:9 * k + 9])

    solve(slabs, rate, offset, store)


def cycle_later_kernel(slabs, both, offset, jump, out, jump_out, sem):
    copy = pltpu.make_async_copy(jump, jump_out, sem)
    copy.start()

    def store(k, u):
        out[k] = u

    solve(slabs, lambda k: both[9 * k + 1:9 * k + 5], lambda k: offset[k], store)
    copy.wait()


SWAP = [(0, 1), (1, 0)]


def spread(x, slabs):
    x = x.reshape(slabs, x.shape[0] // slabs, 1, COLS)
    return lax.all_to_all(x, "tm", 0, 0, tiled=True).reshape(-1, COLS)


def shards(initial_states, coarse_decay, power_map, power_mask, region_ids, region_conductivity):
    slabs = lax.axis_size("tm")
    states, powers, decay = (
        x.reshape(LAYERS * ROWS, COLS) for x in (initial_states, power_map, coarse_decay)
    )
    mask = power_mask[0]

    far = lax.ppermute(states, "sx", SWAP)
    power_far = lax.ppermute(powers, "sx", SWAP)
    start, power_own, rate = call(
        load_kernel,
        [plane(ROWS)] * 3,
        [],
        [pltpu.with_memory_space_constraint(x, pltpu.HBM) for x in (states, powers, decay)],
        "load",
        [VMEM((3, LAYERS * ROWS, COLS), jnp.float32), pltpu.SemaphoreType.DMA((3,))],
        pl.CostEstimate(flops=2_000_000, bytes_accessed=800_000, transcendentals=0),
        pltpu.HBM,
    )
    sent = call(pack_kernel, plane(2 * SENT + THIN), [], [start, far, power_own, power_far, rate], "pack")
    other = lax.ppermute(sent, "sy", SWAP)
    end, base, heat, power, band, power_band = call(
        tile_kernel,
        [plane(n) for n in (ROWS, BLOCKS, FSTEPS * BLOCKS, BOX, PACK, PACK)],
        [mask, region_ids, region_conductivity],
        [start, far, power_own, power_far],
        "propagate_tile",
        work_of(BOX),
        pl.CostEstimate(flops=20_000_000, bytes_accessed=4_000_000, transcendentals=400_000),
    )
    power_band, offset, both = call(
        band_kernel,
        [plane(PACK), plane(ROWS), flat(576)],
        [],
        [end, start, rate, base, heat, band, power_band, other],
        "propagate_band",
        [VMEM((PACK, LAYERS, COLS), jnp.float32)] + work_of(PACK),
    )
    both = spread(both, slabs)
    states = spread(call(functools.partial(cycle_kernel, slabs), flat(320), [], [both], "cycle"), slabs)

    own, send = call(turn_kernel, [plane(ROWS + FRINGE), plane(HALO + FRINGE)], [], [states], "turn")
    far = lax.ppermute(send, "sx", SWAP)
    later, jump = call(
        later_kernel,
        [flat(256), flat(256)],
        [],
        [own, far, rate, base, heat, power, power_band, offset],
        "propagate_later",
        work_of(BOX) + work_of(PACK),
    )
    later = lax.all_to_all(later.reshape(slabs, 4, COLS), "tm", 0, 0, tiled=True)
    states, jump = pl.pallas_call(
        functools.partial(cycle_later_kernel, slabs),
        out_shape=[jax.ShapeDtypeStruct((slabs, 4, COLS), jnp.float32), flat(LAYERS * ROWS)],
        in_specs=[spec()] * 3,
        out_specs=[spec(), pl.BlockSpec(memory_space=pl.ANY)],
        scratch_shapes=[pltpu.SemaphoreType.DMA],
        compiler_params=pltpu.CompilerParams(vmem_limit_bytes=8 * 1024 * 1024),
        name="cycle_later",
    )(both, later, jump)
    states = lax.all_to_all(states, "tm", 0, 0, tiled=True)
    shape = (1, LAYERS, ROWS, COLS)
    return states.reshape(shape), jump.reshape(shape)


def solution(mesh):
    return jax.shard_map(
        shards,
        mesh=mesh,
        in_specs=(
            P("tm", None, "sx", "sy"),
            P("tm", None, "sx", "sy"),
            P(None, "sx", "sy"),
            P("tm", None, None),
            P(),
            P(),
        ),
        out_specs=(P("tm", None, "sx", "sy"), P("tm", None, "sx", "sy")),
        check_vma=False,
    )
```

```python
import functools

import jax
import jax.numpy as jnp
from jax import lax
from jax.experimental import pallas as pl
from jax.experimental.pallas import tpu as pltpu
from jax.sharding import PartitionSpec as P

RB = 8
REGIONS = 4
FSTEPS = 4
SWEEPS = 3
ITERS = 2
cond_slope = 0.25
joule_slope = 0.3

HALO = FSTEPS * SWEEPS
ROWS = 32
LAYERS = 8
COLS = 128
BOX = ROWS + HALO
EDGE = 2 * HALO
WIDE = 64
PACK = 22
BLOCKS = 6
SENT = 9
THIN = 4
FRINGE = 8
VMEM = pltpu.VMEM


def spec():
    return pl.BlockSpec(memory_space=VMEM)


def sspec():
    return pl.BlockSpec(memory_space=pltpu.SMEM)


def plane(*shape):
    return jax.ShapeDtypeStruct((*shape, LAYERS, COLS), jnp.float32)


def flat(rows):
    return jax.ShapeDtypeStruct((rows, COLS), jnp.float32)


def call(kernel, outs, scalars, arrays, name, work=(), cost=None, place=VMEM):
    single = not isinstance(outs, list)
    return pl.pallas_call(
        kernel,
        out_shape=outs,
        in_specs=[sspec()] * len(scalars) + [pl.BlockSpec(memory_space=place)] * len(arrays),
        out_specs=spec() if single else [spec()] * len(outs),
        scratch_shapes=list(work),
        cost_estimate=cost,
        compiler_params=pltpu.CompilerParams(vmem_limit_bytes=8 * 1024 * 1024),
        name=name,
    )(*scalars, *arrays)


def lanes():
    return lax.broadcasted_iota(jnp.int32, (LAYERS, COLS), 1)


def layers():
    return lax.broadcasted_iota(jnp.int32, (LAYERS, COLS), 0)


def moved(value, known, unknown=None):
    known = known % COLS
    if unknown is None:
        return pltpu.roll(value, known, 1) if known else value
    return pltpu.roll(value, (unknown + known) & (COLS - 1), 1)


def position():
    return lax.axis_index("sx"), lax.axis_index("sy")


def native_row(here, r):
    return jnp.where(here[0] == 0, r, ROWS - 1 - r)


def native(here, ref, r):
    return ref[pl.ds(native_row(here, r), LAYERS, stride=ROWS), :]


def place_of(here, r, size):
    up, down = (x // 4 * size + 1 + x % 4 for x in (r, ROWS - 1 - r))
    return jnp.where(here[0] == 0, up, down)


def box_row(here, own, far, r):
    return own[r] if r < ROWS else native(here, far, r - ROWS)


def load_kernel(*refs):
    here = position()
    arrays, outs, held, sem = refs[:3], refs[3:6], refs[6], refs[7]
    copies = [pltpu.make_async_copy(arrays[k], held.at[k], sem.at[k]) for k in range(3)]
    for copy in copies:
        copy.start()
    for k in range(3):
        copies[k].wait()
        for r in range(ROWS):
            outs[k][r] = native(here, held.at[k], r)


def banded(i, row):
    return jnp.where(lanes() < WIDE, moved(row(i), EDGE), moved(row(PACK + i), EDGE + WIDE))


class Part:
    def __init__(self, n, packed, power, base, heat, work):
        self.n, self.packed, self.power, self.base, self.heat = n, packed, power, base, heat
        self.state, self.wx, self.wyp, self.wzp, self.inv, self.rhs = work

    def prepare(self, m, now, old, coef_now, coef_old, half):
        n, packed = self.n, self.packed
        lane = lanes()
        layer = layers()
        edge = jnp.where(layer == 0, 1.0, 0.0)
        if not packed:
            edge = edge + jnp.where(lane == 0, 1.0, 0.0) + jnp.where(lane == COLS - 1, 1.0, 0.0)
        cond = []
        for r in range(n):
            cur = self.state[now, r]
            tanh = jnp.tanh(cur)
            cond.append((half * self.base(r)) * (1.0 - cond_slope * tanh))
            source = (half * self.heat(m, r)) * self.power[r] * (1.0 + joule_slope * tanh)
            if m:
                self.rhs[r] = (coef_now * cur + coef_old * self.state[old, r]) + source
            else:
                self.rhs[r] = cur + source
        faces = [None] * (n + 1)
        for r in range(1, n):
            faces[r] = cond[r - 1] + cond[r]
        if packed:
            faces[0] = jnp.where(lane < WIDE, 0.0, cond[0] + moved(cond[n - 1], WIDE))
            faces[n] = cond[n - 1] + moved(cond[0], WIDE)
        for r in range(n):
            c = cond[r]
            north = c + moved(c, -1)
            if not packed:
                north = jnp.where(lane == COLS - 1, 0.0, north)
            up = jnp.where(layer == LAYERS - 1, 0.0, 0.5 * (c + pltpu.roll(c, LAYERS - 1, 0)))
            total = (north + moved(north, 1)) + (up + pltpu.roll(up, 1, 0)) + (1.0 + edge * c)
            low = faces[r]
            if r == 0:
                low = c if low is None else low + jnp.where(lane < WIDE, c, 0.0)
            high = c if faces[r + 1] is None else faces[r + 1]
            self.wyp[r] = north
            self.wzp[r] = up
            self.inv[r] = 1.0 / (total + (low + high))
        for r in range(n + 1):
            if faces[r] is not None:
                self.wx[r] = faces[r]

    def sweep(self, vs):
        n, packed = self.n, self.packed
        out = []
        for r in range(n):
            v = vs[r]
            north = self.wyp[r]
            up = self.wzp[r]
            across = north * moved(v, -1) + moved(north * v, 1)
            along = up * pltpu.roll(v, LAYERS - 1, 0) + pltpu.roll(up * v, 1, 0)
            acc = self.rhs[r]
            if r:
                acc = acc + self.wx[r] * vs[r - 1]
            elif packed:
                acc = acc + self.wx[0] * moved(vs[n - 1], WIDE)
            if r < n - 1:
                acc = acc + self.wx[r + 1] * vs[r + 1]
            elif packed:
                acc = acc + self.wx[n] * moved(vs[0], WIDE)
            out.append((acc + (across + along)) * self.inv[r])
        return out


def advance(*parts):
    for m in range(FSTEPS):
        now = m % 2
        old = 1 - now
        coefs = (4.0 / 3.0, -1.0 / 3.0, 1.0 / 3.0) if m else (1.0, 0.0, 0.5)
        for part in parts:
            part.prepare(m, now, old, *coefs)
        values = [[part.state[now, r] for r in range(part.n)] for part in parts]
        for k in range(SWEEPS):
            values = [part.sweep(vs) for part, vs in zip(parts, values)]
        for part, vs in zip(parts, values):
            for r in range(part.n):
                part.state[old, r] = vs[r]


def work_of(n):
    return [VMEM((2, n, LAYERS, COLS), jnp.float32)] + [VMEM((n + 1, LAYERS, COLS), jnp.float32)] * 5


def turned(here, block):
    return jnp.where(here[0] == 0, block, 7 - block)


def tile_part(base, heat, power, work):
    return Part(BOX, False, power, lambda r: base[r // RB], lambda m, r: heat[m * BLOCKS + r // RB], work)


def band_part(base, heat, power, work):
    low = lanes() < WIDE

    def two(ref, first, i):
        return jnp.where(low, ref[first + i // RB], ref[first + (i + PACK) // RB])

    return Part(PACK, True, power, lambda i: two(base, 0, i), lambda m, i: two(heat, m * BLOCKS, i), work)


def pack_kernel(own, far, power_own, power_far, rate, out):
    here = position()
    left = here[1] == 0
    lane = lanes()
    edge = jnp.where(left, EDGE, 0)
    fringe = jnp.where(left, HALO, 0)
    for k, (near, other) in enumerate(((own, far), (power_own, power_far))):
        for i in range(SENT):
            value = None
            for q in range(5):
                r = min(q * SENT + i, BOX - 1)
                part = moved(box_row(here, near, other, r), q * EDGE, edge)
                value = part if value is None else jnp.where(lane < q * EDGE, value, part)
            out[k * SENT + i] = value
    for i in range(THIN):
        value = None
        for q in range(8):
            part = moved(rate[q * THIN + i], q * 16, fringe)
            value = part if value is None else jnp.where(lane < q * 16, value, part)
        out[2 * SENT + i] = value


def tile_kernel(mask, ids, conductivity, own, far, power_own, power_far, *refs):
    here = position()
    end, base, heat, power, band, power_band, *work = refs
    state = work[0]
    layer = layers()
    for b in range(BLOCKS):
        value = jnp.zeros((LAYERS, COLS), jnp.float32)
        for l in range(LAYERS):
            value = jnp.where(layer == l, conductivity[ids[l, turned(here, b)]], value)
        base[b] = value
        for m in range(FSTEPS):
            on = mask[m, turned(here, b)].astype(jnp.float32)
            heat[m * BLOCKS + b] = jnp.full((LAYERS, COLS), on, jnp.float32)
    for r in range(BOX):
        row = box_row(here, own, far, r)
        state[0, r] = row
        power[r] = box_row(here, power_own, power_far, r)
    for i in range(PACK):
        band[i] = banded(i, lambda r: state[0, r])
        power_band[i] = banded(i, lambda r: power[r])
    advance(tile_part(base, heat, power, work))
    for r in range(ROWS):
        end[r] = state[0, r]


def fringe_shift(left):
    return jnp.where(left, EDGE, HALO)


def merged(here, r, state, end):
    lane = lanes()
    left = here[1] == 0
    border = ((lane >= COLS - HALO) & left) | ((lane < HALO) & jnp.logical_not(left))
    return jnp.where(border, moved(state[0, r % PACK], -EDGE - WIDE * (r // PACK)), end)


def band_kernel(end, start, rate, base, heat, band, power_own, other, *refs):
    here = position()
    power, offset_out, send, first_band, *work = refs
    state = work[0]
    lane = lanes()
    left = here[1] == 0
    mine = ((lane & (WIDE - 1)) < EDGE) == left
    place = jnp.where(left, EDGE, 0)

    def received(k, i):
        parts = []
        for g in range(2):
            r = g * PACK + i
            parts.append(moved(other[k * SENT + r % SENT], g * WIDE - EDGE * (r // SENT), place))
        return jnp.where(lane < WIDE, parts[0], parts[1])

    for i in range(PACK):
        row = jnp.where(mine, band[i], received(0, i))
        state[0, i] = row
        first_band[i] = row
        power[i] = jnp.where(mine, power_own[i], received(1, i))
    advance(band_part(base, heat, power, work))
    for r in range(ROWS):
        d = rate[r]
        offset = merged(here, r, state, end[r]) - d * start[r]
        offset_out[r] = offset
        at = place_of(here, r, 9)
        send[pl.ds(at, LAYERS, stride=72), :] = d
        send[pl.ds(at + 4, LAYERS, stride=72), :] = offset
    back = COLS - fringe_shift(left)
    for j in range(FRINGE):
        first, last = None, None
        for g in range(4):
            r = g * FRINGE + j
            by = g * 32 - WIDE * (r // PACK)
            u = moved(first_band[r % PACK], by, back)
            f = moved(state[0, r % PACK], by, back)
            first = u if g == 0 else jnp.where(lane < g * 32, first, u)
            last = f if g == 0 else jnp.where(lane < g * 32, last, f)
        d = moved(other[2 * SENT + j % THIN], -16 * (j // THIN))
        send[pl.ds(j * 72, LAYERS, stride=9), :] = jnp.where((lane & 31) < 16, d, moved(last - d * first, 16))


def turn_kernel(states, out, send):
    here = position()
    for r in range(ROWS):
        row = states[pl.ds(place_of(here, r, 5), LAYERS, stride=40), :]
        out[r] = row
        if r >= ROWS - HALO:
            send[r - (ROWS - HALO)] = row
    for j in range(FRINGE):
        row = states[pl.ds(j * 40, LAYERS, stride=5), :]
        out[ROWS + j] = row
        send[HALO + j] = row


def later_kernel(own, far, rate, base, heat, power, power_band, offset_before, *refs):
    here = position()
    send, jump, *work = refs
    tile, band = work[:6], work[6:]
    lane = lanes()
    slot = lane & (WIDE - 1)
    left = here[1] == 0
    shift = fringe_shift(left)
    fringe = (slot >= shift) & (slot < shift + HALO)
    def at_start(r):
        return own[r] if r < ROWS else far[BOX - 1 - r]

    for r in range(BOX):
        tile[0][0, r] = at_start(r)
    for i in range(PACK):
        parts = []
        for g in range(2):
            r = g * PACK + i
            source, k, at = (own, r, ROWS) if r < ROWS else (far, 2 * ROWS - 1 - r, HALO)
            parts.append(moved(source[at + k % FRINGE], g * WIDE - 32 * (k // FRINGE), shift))
        beside = jnp.where(lane < WIDE, parts[0], parts[1])
        row = jnp.where(fringe, beside, banded(i, at_start))
        band[0][0, i] = row
    advance(
        tile_part(base, heat, power, tile),
        band_part(base, heat, power_band, band),
    )
    for r in range(ROWS):
        f = merged(here, r, band[0], tile[0][0, r])
        du = rate[r] * own[r]
        x = native_row(here, r)
        send[pl.ds(x, LAYERS, stride=ROWS), :] = f - du
        jump[pl.ds(x, LAYERS, stride=ROWS), :] = f - (du + offset_before[r])


def solve(slabs, rate, offset, store):
    scale = rate(0)
    shift = offset(0)
    for k in range(1, slabs):
        d = rate(k)
        scale = scale * d
        shift = d * shift + offset(k)
    u = shift / (1.0 - scale)
    store(0, u)
    for k in range(slabs - 1):
        u = rate(k) * u + offset(k)
        store(k + 1, u)


def cycle_kernel(slabs, both, out):
    def store(k, u):
        out[5 * k:5 * k + 5] = u

    row = lax.broadcasted_iota(jnp.int32, (5, COLS), 0)
    slot = lax.broadcasted_iota(jnp.int32, (5, COLS), 1) & 31
    empty = (row == 0) & (slot >= HALO)

    def rate(k):
        return jnp.where(empty, 0.0, both[9 * k:9 * k + 5])

    def offset(k):
        return jnp.where(row == 0, moved(both[9 * k:9 * k + 5], -16), both[9 * k + 4:9 * k + 9])

    solve(slabs, rate, offset, store)


def cycle_later_kernel(slabs, both, offset, jump, out, jump_out, sem):
    copy = pltpu.make_async_copy(jump, jump_out, sem)
    copy.start()

    def store(k, u):
        out[k] = u

    solve(slabs, lambda k: both[9 * k + 1:9 * k + 5], lambda k: offset[k], store)
    copy.wait()


SWAP = [(0, 1), (1, 0)]


def spread(x, slabs):
    x = x.reshape(slabs, x.shape[0] // slabs, 1, COLS)
    return lax.all_to_all(x, "tm", 0, 0, tiled=True).reshape(-1, COLS)


def shards(initial_states, coarse_decay, power_map, power_mask, region_ids, region_conductivity):
    slabs = lax.axis_size("tm")
    states, powers, decay = (
        x.reshape(LAYERS * ROWS, COLS) for x in (initial_states, power_map, coarse_decay)
    )
    mask = power_mask[0]

    far = lax.ppermute(states, "sx", SWAP)
    power_far = lax.ppermute(powers, "sx", SWAP)
    start, power_own, rate = call(
        load_kernel,
        [plane(ROWS)] * 3,
        [],
        [pltpu.with_memory_space_constraint(x, pltpu.HBM) for x in (states, powers, decay)],
        "load",
        [VMEM((3, LAYERS * ROWS, COLS), jnp.float32), pltpu.SemaphoreType.DMA((3,))],
        pl.CostEstimate(flops=2_000_000, bytes_accessed=800_000, transcendentals=0),
        pltpu.HBM,
    )
    sent = call(pack_kernel, plane(2 * SENT + THIN), [], [start, far, power_own, power_far, rate], "pack")
    other = lax.ppermute(sent, "sy", SWAP)
    end, base, heat, power, band, power_band = call(
        tile_kernel,
        [plane(n) for n in (ROWS, BLOCKS, FSTEPS * BLOCKS, BOX, PACK, PACK)],
        [mask, region_ids, region_conductivity],
        [start, far, power_own, power_far],
        "propagate_tile",
        work_of(BOX),
        pl.CostEstimate(flops=20_000_000, bytes_accessed=4_000_000, transcendentals=400_000),
    )
    power_band, offset, both = call(
        band_kernel,
        [plane(PACK), plane(ROWS), flat(576)],
        [],
        [end, start, rate, base, heat, band, power_band, other],
        "propagate_band",
        [VMEM((PACK, LAYERS, COLS), jnp.float32)] + work_of(PACK),
    )
    both = spread(both, slabs)
    states = spread(call(functools.partial(cycle_kernel, slabs), flat(320), [], [both], "cycle"), slabs)

    own, send = call(turn_kernel, [plane(ROWS + FRINGE), plane(HALO + FRINGE)], [], [states], "turn")
    far = lax.ppermute(send, "sx", SWAP)
    later, jump = call(
        later_kernel,
        [flat(256), flat(256)],
        [],
        [own, far, rate, base, heat, power, power_band, offset],
        "propagate_later",
        work_of(BOX) + work_of(PACK),
    )
    later = lax.all_to_all(later.reshape(slabs, 4, COLS), "tm", 0, 0, tiled=True)
    states, jump = pl.pallas_call(
        functools.partial(cycle_later_kernel, slabs),
        out_shape=[jax.ShapeDtypeStruct((slabs, 4, COLS), jnp.float32), flat(LAYERS * ROWS)],
        in_specs=[spec()] * 3,
        out_specs=[spec(), pl.BlockSpec(memory_space=pl.ANY)],
        scratch_shapes=[pltpu.SemaphoreType.DMA],
        compiler_params=pltpu.CompilerParams(vmem_limit_bytes=8 * 1024 * 1024),
        name="cycle_later",
    )(both, later, jump)
    states = lax.all_to_all(states, "tm", 0, 0, tiled=True)
    shape = (1, LAYERS, ROWS, COLS)
    return states.reshape(shape), jump.reshape(shape)


def solution(mesh):
    return jax.shard_map(
        shards,
        mesh=mesh,
        in_specs=(
            P("tm", None, "sx", "sy"),
            P("tm", None, "sx", "sy"),
            P(None, "sx", "sy"),
            P("tm", None, None),
            P(),
            P(),
        ),
        out_specs=(P("tm", None, "sx", "sy"), P("tm", None, "sx", "sy")),
        check_vma=False,
    )
```

```python
import functools

import jax
import jax.numpy as jnp
from jax import lax
from jax.experimental import pallas as pl
from jax.experimental.pallas import tpu as pltpu
from jax.sharding import PartitionSpec as P

RB = 8
REGIONS = 4
FSTEPS = 4
SWEEPS = 3
ITERS = 2
cond_slope = 0.25
joule_slope = 0.3

HALO = FSTEPS * SWEEPS
ROWS = 32
LAYERS = 8
COLS = 128
BOX = ROWS + HALO
EDGE = 2 * HALO
WIDE = 64
PACK = 22
BLOCKS = 6
SENT = 9
THIN = 4
FRINGE = 8
VMEM = pltpu.VMEM


def spec():
    return pl.BlockSpec(memory_space=VMEM)


def sspec():
    return pl.BlockSpec(memory_space=pltpu.SMEM)


def plane(*shape):
    return jax.ShapeDtypeStruct((*shape, LAYERS, COLS), jnp.float32)


def flat(rows):
    return jax.ShapeDtypeStruct((rows, COLS), jnp.float32)


def call(kernel, outs, scalars, arrays, name, work=(), cost=None, place=VMEM):
    single = not isinstance(outs, list)
    return pl.pallas_call(
        kernel,
        out_shape=outs,
        in_specs=[sspec()] * len(scalars) + [pl.BlockSpec(memory_space=place)] * len(arrays),
        out_specs=spec() if single else [spec()] * len(outs),
        scratch_shapes=list(work),
        cost_estimate=cost,
        compiler_params=pltpu.CompilerParams(vmem_limit_bytes=8 * 1024 * 1024),
        name=name,
    )(*scalars, *arrays)


def lanes():
    return lax.broadcasted_iota(jnp.int32, (LAYERS, COLS), 1)


def layers():
    return lax.broadcasted_iota(jnp.int32, (LAYERS, COLS), 0)


def moved(value, known, unknown=None):
    known = known % COLS
    if unknown is None:
        return pltpu.roll(value, known, 1) if known else value
    return pltpu.roll(value, (unknown + known) & (COLS - 1), 1)


def position():
    return lax.axis_index("sx"), lax.axis_index("sy")


def native_row(here, r):
    return jnp.where(here[0] == 0, r, ROWS - 1 - r)


def native(here, ref, r):
    return ref[pl.ds(native_row(here, r), LAYERS, stride=ROWS), :]


def place_of(here, r, size):
    up, down = (x // 4 * size + 1 + x % 4 for x in (r, ROWS - 1 - r))
    return jnp.where(here[0] == 0, up, down)


def box_row(here, own, far, r):
    return own[r] if r < ROWS else native(here, far, r - ROWS)


def load_kernel(*refs):
    here = position()
    arrays, outs, held, sem = refs[:3], refs[3:6], refs[6], refs[7]
    copies = [pltpu.make_async_copy(arrays[k], held.at[k], sem.at[k]) for k in range(3)]
    for copy in copies:
        copy.start()
    for k in range(3):
        copies[k].wait()
        for r in range(ROWS):
            outs[k][r] = native(here, held.at[k], r)


def banded(i, row):
    return jnp.where(lanes() < WIDE, moved(row(i), EDGE), moved(row(PACK + i), EDGE + WIDE))


class Part:
    def __init__(self, n, packed, power, base, heat, work):
        self.n, self.packed, self.power, self.base, self.heat = n, packed, power, base, heat
        self.state, self.wx, self.wyp, self.wzp, self.inv, self.rhs = work

    def prepare(self, m, now, old, coef_now, coef_old, half):
        n, packed = self.n, self.packed
        lane = lanes()
        layer = layers()
        edge = jnp.where(layer == 0, 1.0, 0.0)
        share = jnp.where(layer == LAYERS - 1, 0.0, 0.5)
        if not packed:
            edge = edge + jnp.where(lane == 0, 1.0, 0.0) + jnp.where(lane == COLS - 1, 1.0, 0.0)
        cond = []
        for r in range(n):
            cur = self.state[now, r]
            tanh = jnp.tanh(cur)
            cond.append((half * self.base(r)) * (1.0 - cond_slope * tanh))
            source = (half * self.heat(m, r)) * self.power[r] * (1.0 + joule_slope * tanh)
            if m:
                self.rhs[r] = (coef_now * cur + coef_old * self.state[old, r]) + source
            else:
                self.rhs[r] = cur + source
        faces = [None] * (n + 1)
        for r in range(1, n):
            faces[r] = cond[r - 1] + cond[r]
        if packed:
            faces[0] = jnp.where(lane < WIDE, 0.0, cond[0] + moved(cond[n - 1], WIDE))
            faces[n] = cond[n - 1] + moved(cond[0], WIDE)
        for r in range(n):
            c = cond[r]
            north = c + moved(c, -1)
            if not packed:
                north = jnp.where(lane == COLS - 1, 0.0, north)
            up = share * (c + pltpu.roll(c, LAYERS - 1, 0))
            total = (north + moved(north, 1)) + (up + pltpu.roll(up, 1, 0)) + (1.0 + edge * c)
            low = faces[r]
            if r == 0:
                low = c if low is None else low + jnp.where(lane < WIDE, c, 0.0)
            high = c if faces[r + 1] is None else faces[r + 1]
            self.wyp[r] = north
            self.wzp[r] = up
            self.inv[r] = 1.0 / (total + (low + high))
        for r in range(n + 1):
            if faces[r] is not None:
                self.wx[r] = faces[r]

    def sweep(self, vs):
        n, packed = self.n, self.packed
        out = []
        for r in range(n):
            v = vs[r]
            north = self.wyp[r]
            up = self.wzp[r]
            across = north * moved(v, -1) + moved(north * v, 1)
            along = up * pltpu.roll(v, LAYERS - 1, 0) + pltpu.roll(up * v, 1, 0)
            acc = self.rhs[r]
            if r:
                acc = acc + self.wx[r] * vs[r - 1]
            elif packed:
                acc = acc + self.wx[0] * moved(vs[n - 1], WIDE)
            if r < n - 1:
                acc = acc + self.wx[r + 1] * vs[r + 1]
            elif packed:
                acc = acc + self.wx[n] * moved(vs[0], WIDE)
            out.append((acc + (across + along)) * self.inv[r])
        return out


def advance(*parts):
    for m in range(FSTEPS):
        now = m % 2
        old = 1 - now
        coefs = (4.0 / 3.0, -1.0 / 3.0, 1.0 / 3.0) if m else (1.0, 0.0, 0.5)
        for part in parts:
            part.prepare(m, now, old, *coefs)
        values = [[part.state[now, r] for r in range(part.n)] for part in parts]
        for k in range(SWEEPS):
            values = [part.sweep(vs) for part, vs in zip(parts, values)]
        for part, vs in zip(parts, values):
            for r in range(part.n):
                part.state[old, r] = vs[r]


def work_of(n):
    return [VMEM((2, n, LAYERS, COLS), jnp.float32)] + [VMEM((n + 1, LAYERS, COLS), jnp.float32)] * 5


def turned(here, block):
    return jnp.where(here[0] == 0, block, 7 - block)


def tile_part(base, heat, power, work):
    return Part(BOX, False, power, lambda r: base[r // RB], lambda m, r: heat[m * BLOCKS + r // RB], work)


def band_part(base, heat, power, work):
    low = lanes() < WIDE

    def two(ref, first, i):
        return jnp.where(low, ref[first + i // RB], ref[first + (i + PACK) // RB])

    return Part(PACK, True, power, lambda i: two(base, 0, i), lambda m, i: two(heat, m * BLOCKS, i), work)


def pack_kernel(own, far, power_own, power_far, rate, out):
    here = position()
    left = here[1] == 0
    lane = lanes()
    edge = jnp.where(left, EDGE, 0)
    fringe = jnp.where(left, HALO, 0)
    for k, (near, other) in enumerate(((own, far), (power_own, power_far))):
        for i in range(SENT):
            value = None
            for q in range(5):
                r = min(q * SENT + i, BOX - 1)
                part = moved(box_row(here, near, other, r), q * EDGE, edge)
                value = part if value is None else jnp.where(lane < q * EDGE, value, part)
            out[k * SENT + i] = value
    for i in range(THIN):
        value = None
        for q in range(8):
            part = moved(rate[q * THIN + i], q * 16, fringe)
            value = part if value is None else jnp.where(lane < q * 16, value, part)
        out[2 * SENT + i] = value


def tile_kernel(mask, ids, conductivity, own, far, power_own, power_far, *refs):
    here = position()
    end, base, heat, power, band, power_band, *work = refs
    state = work[0]
    layer = layers()
    for b in range(BLOCKS):
        value = jnp.zeros((LAYERS, COLS), jnp.float32)
        for l in range(LAYERS):
            value = jnp.where(layer == l, conductivity[ids[l, turned(here, b)]], value)
        base[b] = value
        for m in range(FSTEPS):
            on = mask[m, turned(here, b)].astype(jnp.float32)
            heat[m * BLOCKS + b] = jnp.full((LAYERS, COLS), on, jnp.float32)
    for r in range(BOX):
        row = box_row(here, own, far, r)
        state[0, r] = row
        power[r] = box_row(here, power_own, power_far, r)
    for i in range(PACK):
        band[i] = banded(i, lambda r: state[0, r])
        power_band[i] = banded(i, lambda r: power[r])
    advance(tile_part(base, heat, power, work))
    for r in range(ROWS):
        end[r] = state[0, r]


def fringe_shift(left):
    return jnp.where(left, EDGE, HALO)


def merged(here, r, state, end):
    lane = lanes()
    left = here[1] == 0
    border = ((lane >= COLS - HALO) & left) | ((lane < HALO) & jnp.logical_not(left))
    return jnp.where(border, moved(state[0, r % PACK], -EDGE - WIDE * (r // PACK)), end)


def band_kernel(end, start, rate, base, heat, band, power_own, other, *refs):
    here = position()
    power, offset_out, send, first_band, *work = refs
    state = work[0]
    lane = lanes()
    left = here[1] == 0
    mine = ((lane & (WIDE - 1)) < EDGE) == left
    place = jnp.where(left, EDGE, 0)

    def received(k, i):
        parts = []
        for g in range(2):
            r = g * PACK + i
            parts.append(moved(other[k * SENT + r % SENT], g * WIDE - EDGE * (r // SENT), place))
        return jnp.where(lane < WIDE, parts[0], parts[1])

    for i in range(PACK):
        row = jnp.where(mine, band[i], received(0, i))
        state[0, i] = row
        first_band[i] = row
        power[i] = jnp.where(mine, power_own[i], received(1, i))
    advance(band_part(base, heat, power, work))
    for r in range(ROWS):
        d = rate[r]
        offset = merged(here, r, state, end[r]) - d * start[r]
        offset_out[r] = offset
        at = place_of(here, r, 9)
        send[pl.ds(at, LAYERS, stride=72), :] = d
        send[pl.ds(at + 4, LAYERS, stride=72), :] = offset
    back = COLS - fringe_shift(left)
    for j in range(FRINGE):
        first, last = None, None
        for g in range(4):
            r = g * FRINGE + j
            by = g * 32 - WIDE * (r // PACK)
            u = moved(first_band[r % PACK], by, back)
            f = moved(state[0, r % PACK], by, back)
            first = u if g == 0 else jnp.where(lane < g * 32, first, u)
            last = f if g == 0 else jnp.where(lane < g * 32, last, f)
        d = moved(other[2 * SENT + j % THIN], -16 * (j // THIN))
        send[pl.ds(j * 72, LAYERS, stride=9), :] = jnp.where((lane & 31) < 16, d, moved(last - d * first, 16))


def turn_kernel(states, out, send):
    here = position()
    for r in range(ROWS):
        row = states[pl.ds(place_of(here, r, 5), LAYERS, stride=40), :]
        out[r] = row
        if r >= ROWS - HALO:
            send[r - (ROWS - HALO)] = row
    for j in range(FRINGE):
        row = states[pl.ds(j * 40, LAYERS, stride=5), :]
        out[ROWS + j] = row
        send[HALO + j] = row


def later_kernel(own, far, rate, base, heat, power, power_band, offset_before, *refs):
    here = position()
    send, jump, *work = refs
    tile, band = work[:6], work[6:]
    lane = lanes()
    slot = lane & (WIDE - 1)
    left = here[1] == 0
    shift = fringe_shift(left)
    fringe = (slot >= shift) & (slot < shift + HALO)
    for r in range(BOX):
        row = own[r] if r < ROWS else far[BOX - 1 - r]
        tile[0][0, r] = row
    for i in range(PACK):
        parts = []
        for g in range(2):
            r = g * PACK + i
            source, k, at = (own, r, ROWS) if r < ROWS else (far, 2 * ROWS - 1 - r, HALO)
            parts.append(moved(source[at + k % FRINGE], g * WIDE - 32 * (k // FRINGE), shift))
        beside = jnp.where(lane < WIDE, parts[0], parts[1])
        row = jnp.where(fringe, beside, banded(i, lambda r: tile[0][0, r]))
        band[0][0, i] = row
    advance(
        tile_part(base, heat, power, tile),
        band_part(base, heat, power_band, band),
    )
    for r in range(ROWS):
        f = merged(here, r, band[0], tile[0][0, r])
        du = rate[r] * own[r]
        x = native_row(here, r)
        send[pl.ds(x, LAYERS, stride=ROWS), :] = f - du
        jump[pl.ds(x, LAYERS, stride=ROWS), :] = f - (du + offset_before[r])


def solve(slabs, rate, offset, store):
    scale = rate(0)
    shift = offset(0)
    for k in range(1, slabs):
        d = rate(k)
        scale = scale * d
        shift = d * shift + offset(k)
    u = shift / (1.0 - scale)
    store(0, u)
    for k in range(slabs - 1):
        u = rate(k) * u + offset(k)
        store(k + 1, u)


def cycle_kernel(slabs, both, out):
    def store(k, u):
        out[5 * k:5 * k + 5] = u

    row = lax.broadcasted_iota(jnp.int32, (5, COLS), 0)
    slot = lax.broadcasted_iota(jnp.int32, (5, COLS), 1) & 31
    empty = (row == 0) & (slot >= HALO)

    def rate(k):
        return jnp.where(empty, 0.0, both[9 * k:9 * k + 5])

    def offset(k):
        return jnp.where(row == 0, moved(both[9 * k:9 * k + 5], -16), both[9 * k + 4:9 * k + 9])

    solve(slabs, rate, offset, store)


def cycle_later_kernel(slabs, both, offset, jump, out, jump_out, sem):
    copy = pltpu.make_async_copy(jump, jump_out, sem)
    copy.start()

    def store(k, u):
        out[k] = u

    solve(slabs, lambda k: both[9 * k + 1:9 * k + 5], lambda k: offset[k], store)
    copy.wait()


SWAP = [(0, 1), (1, 0)]


def spread(x, slabs):
    x = x.reshape(slabs, x.shape[0] // slabs, 1, COLS)
    return lax.all_to_all(x, "tm", 0, 0, tiled=True).reshape(-1, COLS)


def shards(initial_states, coarse_decay, power_map, power_mask, region_ids, region_conductivity):
    slabs = lax.axis_size("tm")
    states, powers, decay = (
        x.reshape(LAYERS * ROWS, COLS) for x in (initial_states, power_map, coarse_decay)
    )
    mask = power_mask[0]

    far = lax.ppermute(states, "sx", SWAP)
    power_far = lax.ppermute(powers, "sx", SWAP)
    start, power_own, rate = call(
        load_kernel,
        [plane(ROWS)] * 3,
        [],
        [pltpu.with_memory_space_constraint(x, pltpu.HBM) for x in (states, powers, decay)],
        "load",
        [VMEM((3, LAYERS * ROWS, COLS), jnp.float32), pltpu.SemaphoreType.DMA((3,))],
        pl.CostEstimate(flops=2_000_000, bytes_accessed=800_000, transcendentals=0),
        pltpu.HBM,
    )
    sent = call(pack_kernel, plane(2 * SENT + THIN), [], [start, far, power_own, power_far, rate], "pack")
    other = lax.ppermute(sent, "sy", SWAP)
    end, base, heat, power, band, power_band = call(
        tile_kernel,
        [plane(n) for n in (ROWS, BLOCKS, FSTEPS * BLOCKS, BOX, PACK, PACK)],
        [mask, region_ids, region_conductivity],
        [start, far, power_own, power_far],
        "propagate_tile",
        work_of(BOX),
        pl.CostEstimate(flops=20_000_000, bytes_accessed=4_000_000, transcendentals=400_000),
    )
    power_band, offset, both = call(
        band_kernel,
        [plane(PACK), plane(ROWS), flat(576)],
        [],
        [end, start, rate, base, heat, band, power_band, other],
        "propagate_band",
        [VMEM((PACK, LAYERS, COLS), jnp.float32)] + work_of(PACK),
    )
    both = spread(both, slabs)
    states = spread(call(functools.partial(cycle_kernel, slabs), flat(320), [], [both], "cycle"), slabs)

    own, send = call(turn_kernel, [plane(ROWS + FRINGE), plane(HALO + FRINGE)], [], [states], "turn")
    far = lax.ppermute(send, "sx", SWAP)
    later, jump = call(
        later_kernel,
        [flat(256), flat(256)],
        [],
        [own, far, rate, base, heat, power, power_band, offset],
        "propagate_later",
        work_of(BOX) + work_of(PACK),
    )
    later = lax.all_to_all(later.reshape(slabs, 4, COLS), "tm", 0, 0, tiled=True)
    states, jump = pl.pallas_call(
        functools.partial(cycle_later_kernel, slabs),
        out_shape=[jax.ShapeDtypeStruct((slabs, 4, COLS), jnp.float32), flat(LAYERS * ROWS)],
        in_specs=[spec()] * 3,
        out_specs=[spec(), pl.BlockSpec(memory_space=pl.ANY)],
        scratch_shapes=[pltpu.SemaphoreType.DMA],
        compiler_params=pltpu.CompilerParams(vmem_limit_bytes=8 * 1024 * 1024),
        name="cycle_later",
    )(both, later, jump)
    states = lax.all_to_all(states, "tm", 0, 0, tiled=True)
    shape = (1, LAYERS, ROWS, COLS)
    return states.reshape(shape), jump.reshape(shape)


def solution(mesh):
    return jax.shard_map(
        shards,
        mesh=mesh,
        in_specs=(
            P("tm", None, "sx", "sy"),
            P("tm", None, "sx", "sy"),
            P(None, "sx", "sy"),
            P("tm", None, None),
            P(),
            P(),
        ),
        out_specs=(P("tm", None, "sx", "sy"), P("tm", None, "sx", "sy")),
        check_vma=False,
    )
```
